128 devices in a mesh: box: 16 (over y, x), pair: 8 (over z, core).
Axes of the slice: x: 4, y: 4, z: 4, core: 2. Of those that a mesh axis runs over, the one named last changes fastest.
Arguments:
- multipoles: bfloat16 [441, 262144], P(None, ('box', 'pair')), may hold values from -0.5 to 0.5
- density: float32 [262144], P(('box', 'pair')), may hold values from -0.6 to 0.6
- pair_centers: float32 [3, 262144], P(None, ('box', 'pair')), may hold values from 0 to 4
- pair_exponent: float32 [262144], P(('box', 'pair')), may hold values from 0.3 to 6
- box_of_pair: int32 [262144], P(('box', 'pair')), may hold values from 0 to 32767, as said below
- near_tiles: int32 [2048, 24], P(('box', 'pair')), may hold values from 0 to 2047, as said below
- near_count: int32 [2048], P(('box', 'pair')), may hold values from 1 to 24, as said below
- m2l_source: int32 [32768, 16], P('box'), may hold values from -1 to 32767, as said below
- coarse_source: int32 [512, 16], P('box'), may hold values from -1 to 511, as said below
- m2m_ops: bfloat16 [8, 441, 441], replicated, may hold values from -0.109375 to 0.109375
- l2l_ops: bfloat16 [8, 441, 441], replicated, may hold values from -0.25 to 0.25
- m2l_ops: bfloat16 [16, 441, 441], replicated, may hold values from -0.25 to 0.25
Outputs:
- coulomb: float32 [262144], P(('box', 'pair'))
The draws below stay inside these ranges and needn't reach their ends.
Inputs may be any that keep to these rules, and one draw needn't show every extreme that they name: `box_of_pair`: pairs are sorted by leaf box; the i-th run of 2048 pairs has its leaf boxes in leaves i * 256 to i * 256 + 255. `near_tiles`: the source tiles of a tile lie in the tiles of its own box index or of the box index just before or after it. Only the first near_count[u] entries of row u of near_tiles count; some tile has 24 in every draw. `m2l_source`: -1 marks an absent class; a source is never the target and lies in the block of 2048 leaf boxes of the target's box index or of the box index just before or after it. `coarse_source`: -1 marks an absent class; a source is never the target.
All inputs are finite; a program needn't handle non-finite values.
Results may differ from the reference program's by a relative error of at most 0.0027.
Values may be sent and summed in bfloat16 or wider, within the bound.
A program may use at most 128 MiB of HBM per device.

```python
import math
import jax
import jax.numpy as jnp
from jax import lax

P_SIZE = 441
NCLASS = 16
TILE = 128
NNEAR = 24
LB = 2048
LS = 256
PD = 2048
NLEAF = 32768
NCB = 512
GT = 128
NTILE = 2048
NPAIR = 262144
N_BOX = 16


def draw_box_of_pair(key, part):
    key = jax.random.fold_in(key, 5)
    runs = NPAIR // PD
    within_run = jax.random.randint(key, (runs, PD), 0, LS)
    within_run = jnp.sort(within_run, axis=1)
    run_start = jnp.arange(runs, dtype=jnp.int32) * LS
    return (run_start[:, None] + within_run).reshape(NPAIR).astype(jnp.int32)


def draw_near_tiles(key, part):
    key = jax.random.fold_in(key, 21)
    first, second = jax.random.split(key)
    blocks = NTILE // GT
    target_block = jnp.arange(NTILE, dtype=jnp.int32) // GT
    offsets = jax.random.randint(first, (NTILE, NNEAR), -1, 2)
    source_block = jnp.clip(target_block[:, None] + offsets, 0, blocks - 1)
    within_block = jax.random.randint(second, (NTILE, NNEAR), 0, GT)
    return (source_block * GT + within_block).astype(jnp.int32)


def draw_near_count(key, part):
    key = jax.random.fold_in(key, 37)
    first, second, third = jax.random.split(key, 3)
    blocks = NTILE // GT
    block_load = jax.random.randint(first, (blocks,), 2, NNEAR + 1)
    tile_load = jnp.repeat(block_load, GT)
    counts = 1 + jax.random.randint(second, (NTILE,), 0, 1048576) % tile_load
    forced = jax.random.randint(third, (), 0, NTILE)
    counts = jnp.where(jnp.arange(NTILE, dtype=jnp.int32) == forced, NNEAR, counts)
    return counts.astype(jnp.int32)


def draw_m2l_source(key, part):
    key = jax.random.fold_in(key, 53)
    first, second, third = jax.random.split(key, 3)
    blocks = NLEAF // LB
    target_box = jnp.arange(NLEAF, dtype=jnp.int32)
    target_block = target_box // LB
    offsets = jax.random.randint(first, (NLEAF, NCLASS), -1, 2)
    source_block = jnp.clip(target_block[:, None] + offsets, 0, blocks - 1)
    within_block = jax.random.randint(second, (NLEAF, NCLASS), 0, LB)
    source = source_block * LB + within_block
    source = jnp.where(source == target_box[:, None], jnp.bitwise_xor(source, 1), source)
    absent = jax.random.randint(third, (NLEAF, NCLASS), 0, 8) == 0
    return jnp.where(absent, -1, source).astype(jnp.int32)


def draw_coarse_source(key, part):
    key = jax.random.fold_in(key, 71)
    first, second = jax.random.split(key)
    target_box = jnp.arange(NCB, dtype=jnp.int32)
    source = jax.random.randint(first, (NCB, NCLASS), 0, NCB)
    source = jnp.where(source == target_box[:, None], jnp.bitwise_xor(source, 1), source)
    absent = jax.random.randint(second, (NCB, NCLASS), 0, 8) == 0
    return jnp.where(absent, -1, source).astype(jnp.int32)


def level_of(stream_key, extent, cuts, low, top_value):
    def one(dim, blocks):
        draws = jax.random.uniform(jax.random.fold_in(jax.random.fold_in(stream_key, 6), dim), (blocks,), jnp.float32, low / len(cuts), top_value / len(cuts))
        return jnp.repeat(jnp.exp(draws), extent[dim] // blocks).reshape((-1,) + (1,) * (len(extent) - dim - 1))

    level = one(*cuts[0])
    for cut in cuts[1:]:
        level = level * one(*cut)
    return level


def normal_values(rng, dims, scale, most, pieces=(), kind=jnp.bfloat16):
    factor_of = level_of(rng, dims, pieces, -0.22, 0.18) if pieces else 1.0
    entries = jax.random.normal(rng, dims, jnp.float32) * scale * factor_of
    return jnp.minimum(jnp.maximum(entries, -most), most).astype(kind)


def setup_inputs(seed: int = 0) -> dict:
    arg_keys = jax.random.split(jax.random.key(seed), 13)
    return {
        "multipoles": normal_values(arg_keys[0], (P_SIZE, NPAIR), (P_SIZE // 4) ** -0.5, 0.5, ((1, 128),)),
        "density": normal_values(arg_keys[1], (NPAIR,), 0.1, 0.6, ((0, 128),), jnp.float32),
        "pair_centers": jnp.clip(4.0 * jax.random.uniform(arg_keys[2], (3, NPAIR), jnp.float32) ** level_of(arg_keys[2], (3, NPAIR), ((1, 128),), -0.2, 0.2), 0.0, 4.0),
        "pair_exponent": jnp.clip(jnp.exp(math.log(6.0) - 2.9957322 * jax.random.uniform(arg_keys[3], (NPAIR,), jnp.float32) ** level_of(arg_keys[3], (NPAIR,), ((0, 128),), -0.2, 0.2)), 0.3, 6.0),
        "box_of_pair": draw_box_of_pair(jax.random.fold_in(arg_keys[12], 71), 0),
        "near_tiles": draw_near_tiles(jax.random.fold_in(arg_keys[12], 71), 0),
        "near_count": draw_near_count(jax.random.fold_in(arg_keys[12], 71), 0),
        "m2l_source": draw_m2l_source(jax.random.fold_in(arg_keys[12], 71), 0),
        "coarse_source": draw_coarse_source(jax.random.fold_in(arg_keys[12], 71), 0),
        "m2m_ops": normal_values(arg_keys[9], (8, P_SIZE, P_SIZE), (8 * P_SIZE) ** -0.5, 0.109375),
        "l2l_ops": normal_values(arg_keys[10], (8, P_SIZE, P_SIZE), P_SIZE ** -0.5, 0.25),
        "m2l_ops": normal_values(arg_keys[11], (NCLASS, P_SIZE, P_SIZE), P_SIZE ** -0.5, 0.25),
    }


cutoff = 0.0001
center_value = 2.0 / math.sqrt(math.pi)

def rounded(values):
    return lax.optimization_barrier(values.astype(jnp.bfloat16)).astype(jnp.float32)

def interact(own_tiles, source_tiles):
    delta_x = own_tiles[0][:, :, None] - source_tiles[0][:, None, :]
    delta_y = own_tiles[1][:, :, None] - source_tiles[1][:, None, :]
    delta_z = own_tiles[2][:, :, None] - source_tiles[2][:, None, :]
    distance = jnp.sqrt(delta_x * delta_x + delta_y * delta_y + delta_z * delta_z)
    target_exp = own_tiles[3][:, :, None]
    source_exp = source_tiles[3][:, None, :]
    reduced = jnp.sqrt(target_exp * source_exp / (target_exp + source_exp))
    argument = reduced * distance
    safe_arg = jnp.where(argument > cutoff, argument, 1.0)
    shape_fn = jnp.where(argument > cutoff, jax.scipy.special.erf(safe_arg) / safe_arg, center_value)
    return lax.optimization_barrier(jnp.sum(reduced * shape_fn * source_tiles[4][:, None, :], axis=2))

def pick_columns(table, source):
    present = source.T >= 0
    picked = jnp.take(table, jnp.maximum(source.T, 0), axis=1)
    return jnp.where(present[None], picked, 0.0)

def reference(multipoles, density, pair_centers, pair_exponent, box_of_pair, near_tiles, near_count, m2l_source, coarse_source, m2m_ops, l2l_ops, m2l_ops):
    moments_all = multipoles.astype(jnp.float32)
    m2m = m2m_ops.astype(jnp.float32)
    l2l = l2l_ops.astype(jnp.float32)
    m2l = m2l_ops.astype(jnp.float32)
    dens_rounded = rounded(density)
    group_pairs = NPAIR // N_BOX
    group_ids = jnp.arange(N_BOX, dtype=jnp.int32)

    def leaf_group(group_id):
        start = (group_id * group_pairs).astype(jnp.int32)
        moments = lax.dynamic_slice_in_dim(moments_all, start, group_pairs, 1)
        dens_rows = lax.dynamic_slice_in_dim(dens_rounded, start, group_pairs, 0)
        boxes = lax.dynamic_slice_in_dim(box_of_pair, start, group_pairs, 0) - (group_id * LB).astype(jnp.int32)
        return jax.ops.segment_sum((moments * dens_rows[None, :]).T, boxes, num_segments=LB).T
    leaf_sum = lax.map(leaf_group, group_ids)
    leaf_sum = jnp.transpose(leaf_sum, (1, 0, 2)).reshape(P_SIZE, NLEAF)
    leaf_moments = rounded(leaf_sum)

    def climb(values):
        return jnp.einsum('opq,qmo->pm', m2m, values.reshape(P_SIZE, -1, 8))

    def descend(values):
        return jnp.einsum('opq,qm->pmo', l2l, values).reshape(P_SIZE, -1)
    middle_moments = rounded(climb(leaf_moments))
    coarse_moments = rounded(climb(middle_moments))
    coarse_locals = rounded(jnp.einsum('cpq,qct->pt', m2l, pick_columns(coarse_moments, coarse_source)))
    middle_locals = rounded(descend(coarse_locals))
    leaf_down = descend(middle_locals)

    def m2l_group(group_id):
        source = lax.dynamic_slice_in_dim(m2l_source, (group_id * LB).astype(jnp.int32), LB, 0)
        return jnp.einsum('cpq,qct->pt', m2l, pick_columns(leaf_moments, source))
    translated = lax.map(m2l_group, group_ids)
    translated = jnp.transpose(translated, (1, 0, 2)).reshape(P_SIZE, NLEAF)
    leaf_locals = rounded(leaf_down + translated)

    def far_group(group_id):
        start = (group_id * group_pairs).astype(jnp.int32)
        moments = lax.dynamic_slice_in_dim(moments_all, start, group_pairs, 1)
        boxes = lax.dynamic_slice_in_dim(box_of_pair, start, group_pairs, 0)
        return lax.optimization_barrier(jnp.sum(moments * jnp.take(leaf_locals, boxes, axis=1), axis=0))
    far_field = lax.map(far_group, group_ids).reshape(NPAIR)
    packed = jnp.concatenate([pair_centers, pair_exponent[None, :], density[None, :]], axis=0)
    tiles_all = packed.reshape(5, NTILE, TILE)

    def near_tile(tile_id):
        own_tiles = lax.dynamic_slice_in_dim(tiles_all, tile_id, 1, 1)
        own_tiles = jnp.broadcast_to(own_tiles, (5, NNEAR, TILE))
        source_tiles = jnp.take(tiles_all, near_tiles[tile_id], axis=1)
        contrib = interact(own_tiles, source_tiles)
        used = jnp.arange(NNEAR, dtype=jnp.int32) < near_count[tile_id]
        return lax.optimization_barrier(jnp.sum(jnp.where(used[:, None], contrib, 0.0), axis=0))
    near_field = lax.map(near_tile, jnp.arange(NTILE, dtype=jnp.int32)).reshape(NPAIR)
    return near_field + far_field
```

```python
import jax
import jax.numpy as jnp
from jax import lax
from jax.experimental import pallas as pl
from jax.experimental.pallas import tpu as pltpu
from jax.sharding import PartitionSpec as P

MESH = pl.DeviceIdType.MESH
NT = (((1,), (1,)), ((), ()))
NN = (((1,), (0,)), ((), ()))
TILE = 128
TILES = 16
NNEAR = 24
COEF = 441
LEAF = 256
NCLASS = 16
BOXES = 16
LEAF_ROWS = 24 * LEAF
COARSE_ROWS = 512
ZERO_PAD = 16
f32, bf16 = jnp.float32, jnp.bfloat16

FIRST = [((0, 0), (0, 1)), ((0, 0), (0, 3)), ((0, 0), (1, 0)), ((0, 0), (-1, 0)), ((0, 0), (0, 2))]
SECOND = [((0, 3), (1, 0)), ((0, 3), (-1, 0)), ((0, 1), (1, 0)), ((0, 1), (-1, 0))]
THIRD_NEAR = [((-1, 3), (0, 1)), ((1, 1), (0, 3))]
THIRD_LEAF = [((-1, 3), (0, 1), 0), ((1, 3), (0, 1), 0), ((-1, 1), (0, 3), 1), ((1, 1), (0, 3), 1)]
ALL_SHARES = [(dx, dz) for dx in (-1, 0, 1) for dz in range(4)]


def split3(values):
    high = values.astype(bf16).astype(f32)
    rest = values - high
    middle = rest.astype(bf16).astype(f32)
    return high, middle, rest - middle


def kernel(
    near_tiles, near_count, coarse_source, mult_hbm, dens_ref, cent_ref, expo_ref, box_ref,
    m2l_source, m2m_hbm, l2l_hbm, m2l_hbm, out_ref,
    mult, m2m, l2l, m2l, idx_vmem, idx, near_tab, feat, leaf_tab, coarse_tab, sc3, onehot, rowidx,
    wide, tall, wd, spread, gat, acc, near_acc,
    loc_sem, near_send, near_recv, leaf_send, leaf_recv, coarse_send, coarse_recv,
):
    box = lax.axis_index("box")
    pair = lax.axis_index("pair")
    y, x = box // 4, box % 4
    z, core = pair // 2, pair % 2

    def slot_of(dx, dz, which):
        return (dx + 1) * 8 + ((z + dz) % 4) * 2 + which

    def near_device(ndx, ndz, flip=0):
        other = core if not flip else 1 - core
        return ((box + ndx + BOXES) % BOXES, ((z + ndz) % 4) * 2 + other)

    def plane_device(dy, dx, dz):
        return (((y + dy) % 4) * 4 + (x + dx) % 4, ((z + dz) % 4) * 2 + core)

    def local(i, src, dst):
        return pltpu.make_async_copy(src, dst, loc_sem.at[i])

    own_cols = pl.ds(pl.multiple_of(pair * LEAF, LEAF), LEAF)
    cp_mult = local(0, mult_hbm, mult)
    cp_m2m = local(1, m2m_hbm, m2m)
    cp_m2l = local(2, m2l_hbm, m2l)
    cp_l2l = local(3, l2l_hbm, l2l)
    cp_idx = local(4, m2l_source.at[:, own_cols], idx_vmem)
    cp_mult.start()
    cp_idx.start()
    cp_m2m.start()
    cp_m2l.start()
    cp_l2l.start()

    partners = [near_device(0, 1), near_device(0, 2), near_device(0, 3), near_device(1, 0)]
    partners += [near_device(-1, 0), near_device(0, 0, 1)]
    partners += [plane_device(0, d, 0) for d in (1, 2, 3)]
    partners += [plane_device(d, 0, 0) for d in (1, 2, 3)]
    barrier = pltpu.get_barrier_semaphore()
    for device in partners:
        pl.semaphore_signal(barrier, inc=1, device_id=device, device_id_type=MESH)

    own_slot = slot_of(0, 0, core)
    for c in range(3):
        for i in range(TILES):
            row = cent_ref[c : c + 1, i * TILE : (i + 1) * TILE] - 2.0
            near_tab[own_slot, c, i : i + 1, :] = row
    near_tab[own_slot, 3] = 1.0 / expo_ref[...]
    near_tab[own_slot, 4] = dens_ref[...]
    pl.semaphore_wait(barrier, len(partners))

    def near_ref(dx, dz, which):
        return near_tab.at[slot_of(dx, dz, which)]

    def leaf_ref(dx, dz, which, half=None):
        base, size = slot_of(dx, dz, which) * LEAF, LEAF
        if half is not None:
            base, size = base + half * (LEAF // 2), LEAF // 2
        return leaf_tab.at[pl.ds(base, size)]

    def near_copy(i, share, hop, flip=0):
        (dx, dz), (ndx, ndz) = share, hop
        return pltpu.make_async_remote_copy(
            src_ref=near_ref(dx, dz, core),
            dst_ref=near_tab.at[(dx - ndx + 1) * 8 + ((z + dz) % 4) * 2 + core],
            send_sem=near_send.at[i], recv_sem=near_recv.at[i],
            device_id=near_device(ndx, ndz, flip), device_id_type=MESH,
        )

    def leaf_copy(i, share, hop, half=None, flip=0):
        (dx, dz), (ndx, ndz) = share, hop
        return pltpu.make_async_remote_copy(
            src_ref=leaf_ref(dx, dz, core, half), dst_ref=leaf_ref(dx - ndx, dz, core, half),
            send_sem=leaf_send.at[i], recv_sem=leaf_recv.at[i],
            device_id=near_device(ndx, ndz, flip), device_id_type=MESH,
        )

    near_first = [near_copy(i, *t) for i, t in enumerate(FIRST)]
    near_second = [near_copy(5 + i, *t) for i, t in enumerate(SECOND)]
    near_third = [near_copy(9 + i, *t) for i, t in enumerate(THIRD_NEAR)]
    near_core = {s: near_copy(11 + i, s, (0, 0), 1) for i, s in enumerate(ALL_SHARES)}
    leaf_first = [leaf_copy(i, *t) for i, t in enumerate(FIRST)]
    leaf_second = [leaf_copy(5 + i, *t) for i, t in enumerate(SECOND)]
    leaf_third = [leaf_copy(9 + i, *t) for i, t in enumerate(THIRD_LEAF)]
    leaf_core = {s: leaf_copy(13 + i, s, (0, 0), None, 1) for i, s in enumerate(ALL_SHARES)}

    for cp in near_first:
        cp.start()
    near_core[(0, 0)].start()

    local_box = box_ref[...] - (box * (8 * LEAF) + pair * LEAF)
    rowidx[...] = (local_box % 8) * 32 + (local_box // 8 % 8) * 4 + local_box // 64
    row_iota = lax.broadcasted_iota(jnp.int32, (LEAF, TILE), 0)
    for i in range(TILES):
        weight = dens_ref[i : i + 1, :].astype(bf16).astype(f32)
        hit = row_iota == rowidx[i : i + 1, :]
        onehot[:, i * TILE : (i + 1) * TILE] = jnp.where(hit, weight, 0.0).astype(bf16)
    leaf_tab[pl.ds(LEAF_ROWS, ZERO_PAD)] = jnp.zeros((ZERO_PAD, 4, TILE), bf16)
    coarse_tab[pl.ds(COARSE_ROWS, ZERO_PAD)] = jnp.zeros((ZERO_PAD, 4, TILE), bf16)
    cp_mult.wait()
    leaf = lax.dot_general(onehot[...], mult[...], NT, preferred_element_type=f32)
    leaf = jnp.concatenate([leaf, jnp.zeros((LEAF, 512 - COEF), f32)], axis=1)
    for c in range(4):
        sc3[:, c, :] = leaf[:, c * TILE : (c + 1) * TILE]
    leaf_tab[pl.ds(own_slot * LEAF, LEAF)] = sc3[...].astype(bf16)
    for cp in leaf_first:
        cp.start()
    leaf_core[(0, 0)].start()

    def near_forward_second():
        near_first[0].wait_recv()
        near_second[0].start()
        near_second[1].start()
        near_core[(0, 3)].start()
        near_first[1].wait_recv()
        near_second[2].start()
        near_second[3].start()
        near_core[(0, 1)].start()
        near_first[2].wait_recv()
        near_core[(-1, 0)].start()
        near_first[3].wait_recv()
        near_core[(1, 0)].start()
        near_first[4].wait_recv()
        near_core[(0, 2)].start()

    def near_forward_third():
        near_second[0].wait_recv()
        near_third[0].start()
        near_core[(-1, 3)].start()
        near_second[3].wait_recv()
        near_third[1].start()
        near_core[(1, 1)].start()
        near_second[1].wait_recv()
        near_core[(1, 3)].start()
        near_second[2].wait_recv()
        near_core[(-1, 1)].start()

    def near_finish():
        near_third[0].wait_recv()
        near_core[(-1, 2)].start()
        near_third[1].wait_recv()
        near_core[(1, 2)].start()
        for cp in near_core.values():
            cp.wait_recv()

    def stream(operators, total, right, dims, columns):
        def chunk(start, size):
            rows = operators[pl.ds(start, size), :]
            result = lax.dot_general(rows, right, dims, preferred_element_type=f32)
            if columns == 256:
                wide[0, pl.ds(start, size), :] = result[:, :TILE]
                wide[1, pl.ds(start, size), :] = result[:, TILE:]
            else:
                tall[pl.ds(start, size), :] = result

        def step(i, carry):
            chunk(pl.multiple_of(i * 512, 512), 512)
            return carry

        whole = total // 512
        lax.fori_loop(0, whole, step, 0)
        if total % 512:
            chunk(whole * 512, total % 512)

    lane = lax.broadcasted_iota(jnp.int32, (COEF, TILE), 1)

    near_forward_second()

    cp_m2m.wait()
    stream(m2m, 8 * COEF, leaf[:, :COEF].astype(bf16), NT, 256)
    total = None
    for o in range(8):
        part = wide[o // 4, pl.ds(o, COEF, stride=8), :]
        part = jnp.where(lane // 32 == o % 4, part, 0.0)
        total = part if total is None else total + part
    total = total + pltpu.roll(total, 64, 1)
    total = total + pltpu.roll(total, 32, 1)
    near_forward_third()
    stream(m2m, 8 * COEF, total.astype(bf16), NN, 128)
    total = None
    for o in range(8):
        part = tall[pl.ds(o, COEF, stride=8), :]
        part = jnp.where(lane % 32 // 4 == o, part, 0.0)
        total = part if total is None else total + part
    for shift in (16, 8, 4):
        total = total + pltpu.roll(total, shift, 1)
    coarse = jnp.concatenate([total, jnp.zeros((512 - COEF, TILE), f32)], axis=0)
    coarse = jnp.transpose(coarse, (1, 0))
    for c in range(4):
        sc3[0:4, c, :] = coarse[0:4, c * TILE : (c + 1) * TILE]
    core_base, y_base, x_base = core * 256, y * 64, x * 16
    coarse_tab[pl.ds(core_base + y_base + x_base + z * 4, 4)] = sc3[0:4].astype(bf16)

    def coarse_copy(i, base, size, device):
        return pltpu.make_async_remote_copy(
            src_ref=coarse_tab.at[pl.ds(base, size)], dst_ref=coarse_tab.at[pl.ds(base, size)],
            send_sem=coarse_send.at[i], recv_sem=coarse_recv.at[i],
            device_id=device, device_id_type=MESH,
        )

    coarse_z = [
        coarse_copy(i, core_base + y_base + x_base + z * 4, 4, plane_device(0, 0, i + 1))
        for i in range(3)
    ]
    coarse_x = [
        coarse_copy(3 + i, core_base + y_base + x_base, 16, plane_device(0, i + 1, 0))
        for i in range(3)
    ]
    coarse_y = [
        coarse_copy(6 + i, core_base + y_base, 64, plane_device(i + 1, 0, 0)) for i in range(3)
    ]
    coarse_c = [coarse_copy(9, core_base, 256, near_device(0, 0, 1))]
    for cp in coarse_z:
        cp.start()

    near_finish()
    def features(s, carry):
        px, py, pz = near_tab[s, 0], near_tab[s, 1], near_tab[s, 2]
        rows = [px, py, pz, px * px + py * py + pz * pz, jnp.ones_like(px)]
        rows += [near_tab[s, 3], near_tab[s, 4], jnp.zeros_like(px)]
        for r, value in enumerate(rows):
            feat[pl.ds(s * TILES, TILES), r, :] = value
        return carry

    lax.fori_loop(0, 24, features, 0)

    def near_tile(u, carry):
        own = feat[own_slot * TILES + u]
        row = lax.broadcasted_iota(jnp.int32, (8, TILE), 0)
        left = jnp.where(row < 3, -2.0 * own, 0.0)
        left = jnp.where(row == 3, 1.0, left)
        left = jnp.where(row == 4, own[3:4, :], left)
        high, middle, low = split3(left)
        left = jnp.concatenate([high, middle, low, high, middle, high], axis=0)
        left = jnp.transpose(left, (1, 0)).astype(bf16)
        inverse = jnp.transpose(jnp.broadcast_to(own[5:6, :], (TILE, TILE)), (1, 0))
        count = near_count[u]

        def one(k):
            tile = near_tiles[u, k] - (box - 1) * (TILES * 8)
            tile = jnp.where(k < count, tile, 0)
            source = feat[tile]
            high, middle, low = split3(source)
            right = jnp.concatenate([high, high, high, middle, middle, low], axis=0).astype(bf16)
            square = lax.dot_general(left, right, NN, preferred_element_type=f32)
            square = jnp.maximum(square, 1e-9)
            weight = jnp.where(k < count, source[6:7, :], 0.0)
            scale = lax.rsqrt(inverse + source[5:6, :])
            reciprocal = lax.rsqrt(square)
            return lax.erf(square * reciprocal * scale) * (reciprocal * weight)

        def step(i, total):
            for j in range(4):
                total = total + one(i * 4 + j)
            return total

        total = lax.fori_loop(0, NNEAR // 4, step, jnp.zeros((TILE, TILE), f32))
        near_acc[pl.ds(u, 1), :] = jnp.transpose(jnp.sum(total, axis=1, keepdims=True), (1, 0))
        return carry


    cp_m2l.wait()
    spread[3] = jnp.zeros((1024, TILE), f32)

    def unmix(start, size):
        source = pl.ds(start * NCLASS, size * NCLASS)
        for c in range(4):
            width = min(TILE, COEF - c * TILE)
            rows = m2l[source, pl.ds(c * TILE, width)].astype(f32)
            spread[c, pl.ds(0, size * NCLASS), pl.ds(0, width)] = rows
        for k in range(NCLASS):
            for c in range(4):
                own = spread[c, pl.ds(k, size, stride=NCLASS), :]
                wd[k, pl.ds(start, size), pl.ds(c * TILE, TILE)] = own.astype(bf16)

    def unmix_step(i, carry):
        unmix(pl.multiple_of(i * 64, 64), 64)
        return carry

    lax.fori_loop(0, 6, unmix_step, 0)
    unmix(384, COEF - 384)

    cp_idx.wait()
    raw = idx_vmem[...]
    rel = jnp.clip(raw - (box - 1) * (8 * LEAF), 0, LEAF_ROWS - 1)
    row = (rel // LEAF) * LEAF + (rel % 8) * 32 + (rel // 8 % 8) * 4 + rel % LEAF // 64
    idx_vmem[...] = jnp.where(raw < 0, LEAF_ROWS, row)
    cp_smem = local(5, idx_vmem, idx)
    cp_smem.start()

    def near_tiles_of(first, last):
        lax.fori_loop(first, last, near_tile, 0)

    for cp in coarse_z:
        cp.wait_recv()
    for cp in coarse_x:
        cp.start()
    leaf_first[0].wait_recv()
    leaf_second[0].start()
    leaf_second[1].start()
    leaf_core[(0, 3)].start()
    leaf_first[1].wait_recv()
    leaf_second[2].start()
    leaf_second[3].start()
    leaf_core[(0, 1)].start()
    near_tiles_of(0, 4)
    for cp in coarse_x:
        cp.wait_recv()
    for cp in coarse_y:
        cp.start()
    leaf_first[2].wait_recv()
    leaf_core[(-1, 0)].start()
    leaf_first[3].wait_recv()
    leaf_core[(1, 0)].start()
    near_tiles_of(4, 8)
    for cp in coarse_y:
        cp.wait_recv()
    coarse_c[0].start()
    for i, share in enumerate([(-1, 3), (1, 3), (-1, 1), (1, 1)]):
        leaf_second[i].wait_recv()
        leaf_third[i].start()
        leaf_core[share].start()
    leaf_first[4].wait_recv()
    leaf_core[(0, 2)].start()
    near_tiles_of(8, 12)
    coarse_c[0].wait_recv()

    for k in range(NCLASS):
        for t in range(4):
            g = coarse_source[k, pair * 4 + t]
            home, member = g >> 5, (g >> 2) & 7
            place = (member & 1) * 256 + home * 16 + (member >> 1) * 4 + (g & 3)
            place = jnp.where(g < 0, COARSE_ROWS, place)
            gat[0, pl.ds((k * 4 + t) * 4, 4), :] = coarse_tab[place].astype(f32)
    picked = [gat[0, pl.ds(c, 64, stride=4), :] for c in range(4)]
    picked = jnp.concatenate(picked, axis=1)
    picked = jnp.concatenate([picked, picked], axis=0).astype(bf16)
    stream(m2l, NCLASS * COEF, picked[:, :COEF], NT, 128)
    total = None
    for k in range(NCLASS):
        part = tall[pl.ds(k, COEF, stride=NCLASS), :]
        part = jnp.where(lane % 64 // 4 == k, part, 0.0)
        total = part if total is None else total + part
    for shift in (32, 16, 8, 4):
        total = total + pltpu.roll(total, shift, 1)

    cp_l2l.wait()
    stream(l2l, 8 * COEF, total.astype(bf16), NN, 128)
    total = None
    for o in range(8):
        part = tall[pl.ds(o, COEF, stride=8), :]
        part = jnp.where(lane % 32 // 4 == o, part, 0.0)
        total = part if total is None else total + part
    stream(l2l, 8 * COEF, total.astype(bf16), NN, 128)
    acc[...] = jnp.zeros((448, LEAF), f32)
    for side in range(2):
        total = None
        for o in range(4):
            part = tall[pl.ds(side * 4 + o, COEF, stride=8), :]
            part = jnp.where(lane // 32 == o, part, 0.0)
            total = part if total is None else total + part
        acc[pl.ds(0, COEF), pl.ds(side * TILE, TILE)] = total

    leaf_third[0].wait_recv()
    leaf_third[2].wait_recv()
    leaf_core[(-1, 2)].start()
    leaf_third[1].wait_recv()
    leaf_third[3].wait_recv()
    leaf_core[(1, 2)].start()
    near_tiles_of(12, 16)
    cp_smem.wait()
    for cp in leaf_core.values():
        cp.wait_recv()

    def leaf_class(k, carry):
        slot = k % 2

        def rows(i, carry2):
            values = []
            for j in range(64):
                column = (j % 4) * 64 + (j % 32 // 4) * 8 + i * 2 + j // 32
                values.append(leaf_tab[idx[k, column]].astype(f32))
            base = pl.multiple_of(i * 256, 256)
            for j in range(64):
                gat[slot, pl.ds(base + j * 4, 4), :] = values[j]
            return carry2

        lax.fori_loop(0, 4, rows, 0)
        picked = [gat[slot, pl.ds(c, LEAF, stride=4), :].astype(bf16) for c in range(4)]
        picked = jnp.concatenate(picked, axis=1)
        acc[...] += lax.dot_general(wd[k], picked, NT, preferred_element_type=f32)
        return carry

    lax.fori_loop(0, NCLASS, leaf_class, 0)

    locals_ = jnp.transpose(acc[...], (1, 0)).astype(bf16)[:, :COEF]
    for q in range(8):
        columns = mult[:, q * 256 : (q + 1) * 256]
        product = lax.dot_general(locals_, columns, NN, preferred_element_type=f32)
        for h in range(2):
            i = q * 2 + h
            hit = row_iota == rowidx[i : i + 1, :]
            far = jnp.where(hit, product[:, h * TILE : (h + 1) * TILE], 0.0)
            far = jnp.sum(far, axis=0, keepdims=True)
            out_ref[i : i + 1, :] = near_acc[i : i + 1, :] + far

    copies = near_first + near_second + near_third + list(near_core.values())
    copies += leaf_first + leaf_second + leaf_third + list(leaf_core.values())
    copies += coarse_z + coarse_x + coarse_y + coarse_c
    for cp in copies:
        cp.wait_send()


def body(
    multipoles, density, pair_centers, pair_exponent, box_of_pair, near_tiles, near_count,
    m2l_source, coarse_source, m2m_ops, l2l_ops, m2l_ops,
):
    def flat(operators):
        return jnp.transpose(operators, (1, 0, 2)).reshape(-1, COEF)

    grid = (TILES, TILE)
    smem = pl.BlockSpec(memory_space=pltpu.SMEM)
    vmem = pl.BlockSpec(memory_space=pltpu.VMEM)
    anywhere = pl.BlockSpec(memory_space=pl.ANY)
    dma = pltpu.SemaphoreType.DMA
    out = pl.pallas_call(
        kernel,
        out_shape=jax.ShapeDtypeStruct(grid, f32),
        in_specs=[smem, smem, smem, anywhere, vmem, vmem, vmem, vmem]
        + [anywhere, anywhere, anywhere, anywhere],
        out_specs=vmem,
        scratch_shapes=[
            pltpu.VMEM((COEF, 2048), bf16),
            pltpu.VMEM((8 * COEF, COEF), bf16),
            pltpu.VMEM((8 * COEF, COEF), bf16),
            pltpu.VMEM((NCLASS * COEF, COEF), bf16),
            pltpu.VMEM((NCLASS, LEAF), jnp.int32),
            pltpu.SMEM((NCLASS, LEAF), jnp.int32),
            pltpu.VMEM((24, 5, TILES, TILE), f32),
            pltpu.VMEM((24 * TILES, 8, TILE), f32),
            pltpu.VMEM((LEAF_ROWS + ZERO_PAD, 4, TILE), bf16),
            pltpu.VMEM((COARSE_ROWS + ZERO_PAD, 4, TILE), bf16),
            pltpu.VMEM((LEAF, 4, TILE), f32),
            pltpu.VMEM((LEAF, 2048), bf16),
            pltpu.VMEM(grid, jnp.int32),
            pltpu.VMEM((2, 8 * COEF, TILE), f32),
            pltpu.VMEM((NCLASS * COEF, TILE), f32),
            pltpu.VMEM((NCLASS, 448, 512), bf16),
            pltpu.VMEM((4, 1024, TILE), f32),
            pltpu.VMEM((2, 1024, TILE), f32),
            pltpu.VMEM((448, LEAF), f32),
            pltpu.VMEM(grid, f32),
            dma((6,)),
            dma((23,)), dma((23,)), dma((25,)), dma((25,)), dma((10,)), dma((10,)),
        ],
        compiler_params=pltpu.CompilerParams(
            collective_id=0, has_side_effects=True, vmem_limit_bytes=60 * 1024 * 1024
        ),
    )(
        near_tiles, near_count, jnp.transpose(coarse_source), multipoles,
        density.reshape(grid), pair_centers, pair_exponent.reshape(grid),
        box_of_pair.reshape(grid), jnp.transpose(m2l_source),
        flat(m2m_ops), flat(l2l_ops), flat(m2l_ops),
    )
    return out.reshape(-1)


def solution(mesh):
    return jax.shard_map(
        body,
        mesh=mesh,
        in_specs=(
            P(None, ("box", "pair")),
            P(("box", "pair")),
            P(None, ("box", "pair")),
            P(("box", "pair")),
            P(("box", "pair")),
            P(("box", "pair"), None),
            P(("box", "pair")),
            P("box", None),
            P("box", None),
            P(),
            P(),
            P(),
        ),
        out_specs=P(("box", "pair")),
        check_vma=False,
    )
```

```python
import jax
import jax.numpy as jnp
from jax import lax
from jax.experimental import pallas as pl
from jax.experimental.pallas import tpu as pltpu
from jax.sharding import PartitionSpec as P

MESH = pl.DeviceIdType.MESH
NT = (((1,), (1,)), ((), ()))
NN = (((1,), (0,)), ((), ()))
TILE = 128
TILES = 16
NNEAR = 24
COEF = 441
LEAF = 256
NCLASS = 16
BOXES = 16
LEAF_ROWS = 24 * LEAF
COARSE_ROWS = 512
ZERO_PAD = 16
CHUNK = 1152
f32, bf16 = jnp.float32, jnp.bfloat16

FIRST = [((0, 0), (0, 1)), ((0, 0), (0, 3)), ((0, 0), (1, 0)), ((0, 0), (-1, 0)), ((0, 0), (0, 2))]
SECOND = [((0, 3), (1, 0)), ((0, 3), (-1, 0)), ((0, 1), (1, 0)), ((0, 1), (-1, 0))]
THIRD_NEAR = [((-1, 3), (0, 1)), ((1, 1), (0, 3))]
THIRD_LEAF = [((-1, 3), (0, 1), 0), ((1, 3), (0, 1), 0), ((-1, 1), (0, 3), 1), ((1, 1), (0, 3), 1)]
ALL_SHARES = [(dx, dz) for dx in (-1, 0, 1) for dz in range(4)]


def split3(values):
    high = values.astype(bf16).astype(f32)
    rest = values - high
    middle = rest.astype(bf16).astype(f32)
    return high, middle, rest - middle


def kernel(
    near_tiles, near_count, coarse_source, mult_hbm, dens_ref, cent_ref, expo_ref, box_ref,
    m2l_source, m2m_hbm, l2l_hbm, m2l_hbm, out_ref,
    mult, m2m, l2l, m2l, idx_vmem, idx, near_tab, feat, leaf_tab, coarse_tab, sc3, onehot, rowidx,
    wide, tall, wd, gat, gat_other, acc, near_acc,
    loc_sem, near_send, near_recv, leaf_send, leaf_recv, coarse_send, coarse_recv,
):
    box = lax.axis_index("box")
    pair = lax.axis_index("pair")
    y, x = box // 4, box % 4
    z, core = pair // 2, pair % 2

    def slot_of(dx, dz, which):
        return (dx + 1) * 8 + ((z + dz) % 4) * 2 + which

    def near_device(ndx, ndz, flip=0):
        other = core if not flip else 1 - core
        return ((box + ndx + BOXES) % BOXES, ((z + ndz) % 4) * 2 + other)

    def plane_device(dy, dx, dz):
        return (((y + dy) % 4) * 4 + (x + dx) % 4, ((z + dz) % 4) * 2 + core)

    def local(i, src, dst):
        return pltpu.make_async_copy(src, dst, loc_sem.at[i])

    own_cols = pl.ds(pl.multiple_of(pair * LEAF, LEAF), LEAF)
    cp_mult = local(0, mult_hbm, mult)
    cp_m2m = local(1, m2m_hbm, m2m)
    cp_m2l = local(2, m2l_hbm, m2l.at[pl.ds(0, NCLASS * COEF)])
    cp_l2l = local(3, l2l_hbm, l2l)
    cp_idx = local(4, m2l_source.at[:, own_cols], idx_vmem)
    cp_mult.start()
    cp_idx.start()
    cp_m2m.start()
    cp_m2l.start()
    cp_l2l.start()

    partners = [near_device(0, 1), near_device(0, 2), near_device(0, 3), near_device(1, 0)]
    partners += [near_device(-1, 0), near_device(0, 0, 1)]
    partners += [plane_device(0, d, 0) for d in (1, 2, 3)]
    partners += [plane_device(d, 0, 0) for d in (1, 2, 3)]
    barrier = pltpu.get_barrier_semaphore()
    for device in partners:
        pl.semaphore_signal(barrier, inc=1, device_id=device, device_id_type=MESH)

    own_slot = slot_of(0, 0, core)
    for c in range(3):
        for i in range(TILES):
            row = cent_ref[c : c + 1, i * TILE : (i + 1) * TILE] - 2.0
            near_tab[own_slot, c, i : i + 1, :] = row
    near_tab[own_slot, 3] = 1.0 / expo_ref[...]
    near_tab[own_slot, 4] = dens_ref[...]
    pl.semaphore_wait(barrier, len(partners))

    def near_ref(dx, dz, which):
        return near_tab.at[slot_of(dx, dz, which)]

    def leaf_ref(dx, dz, which, half=None):
        base, size = slot_of(dx, dz, which) * LEAF, LEAF
        if half is not None:
            base, size = base + half * (LEAF // 2), LEAF // 2
        return leaf_tab.at[pl.ds(base, size)]

    def near_copy(i, share, hop, flip=0):
        (dx, dz), (ndx, ndz) = share, hop
        return pltpu.make_async_remote_copy(
            src_ref=near_ref(dx, dz, core),
            dst_ref=near_tab.at[(dx - ndx + 1) * 8 + ((z + dz) % 4) * 2 + core],
            send_sem=near_send.at[i], recv_sem=near_recv.at[i],
            device_id=near_device(ndx, ndz, flip), device_id_type=MESH,
        )

    def leaf_copy(i, share, hop, half=None, flip=0):
        (dx, dz), (ndx, ndz) = share, hop
        return pltpu.make_async_remote_copy(
            src_ref=leaf_ref(dx, dz, core, half), dst_ref=leaf_ref(dx - ndx, dz, core, half),
            send_sem=leaf_send.at[i], recv_sem=leaf_recv.at[i],
            device_id=near_device(ndx, ndz, flip), device_id_type=MESH,
        )

    near_first = [near_copy(i, *t) for i, t in enumerate(FIRST)]
    near_second = [near_copy(5 + i, *t) for i, t in enumerate(SECOND)]
    near_third = [near_copy(9 + i, *t) for i, t in enumerate(THIRD_NEAR)]
    near_core = {s: near_copy(11 + i, s, (0, 0), 1) for i, s in enumerate(ALL_SHARES)}
    leaf_first = [leaf_copy(i, *t) for i, t in enumerate(FIRST)]
    leaf_second = [leaf_copy(5 + i, *t) for i, t in enumerate(SECOND)]
    leaf_third = [leaf_copy(9 + i, *t) for i, t in enumerate(THIRD_LEAF)]
    leaf_core = {s: leaf_copy(13 + i, s, (0, 0), None, 1) for i, s in enumerate(ALL_SHARES)}

    for cp in near_first:
        cp.start()
    near_core[(0, 0)].start()

    local_box = box_ref[...] - (box * (8 * LEAF) + pair * LEAF)
    rowidx[...] = (local_box % 8) * 32 + (local_box // 8 % 8) * 4 + local_box // 64
    row_iota = lax.broadcasted_iota(jnp.int32, (LEAF, TILE), 0)
    for i in range(TILES):
        weight = dens_ref[i : i + 1, :].astype(bf16).astype(f32)
        hit = row_iota == rowidx[i : i + 1, :]
        onehot[:, i * TILE : (i + 1) * TILE] = jnp.where(hit, weight, 0.0).astype(bf16)
    leaf_tab[pl.ds(LEAF_ROWS, ZERO_PAD)] = jnp.zeros((ZERO_PAD, 4, TILE), bf16)
    coarse_tab[pl.ds(COARSE_ROWS, ZERO_PAD)] = jnp.zeros((ZERO_PAD, 4, TILE), bf16)
    cp_mult.wait()
    leaf = lax.dot_general(onehot[...], mult[...], NT, preferred_element_type=f32)
    leaf = jnp.concatenate([leaf, jnp.zeros((LEAF, 512 - COEF), f32)], axis=1)
    for c in range(4):
        sc3[:, c, :] = leaf[:, c * TILE : (c + 1) * TILE]
    leaf_tab[pl.ds(own_slot * LEAF, LEAF)] = sc3[...].astype(bf16)

    def near_forward_second():
        near_first[0].wait_recv()
        near_second[0].start()
        near_second[1].start()
        near_core[(0, 3)].start()
        near_first[1].wait_recv()
        near_second[2].start()
        near_second[3].start()
        near_core[(0, 1)].start()
        near_first[2].wait_recv()
        near_core[(-1, 0)].start()
        near_first[3].wait_recv()
        near_core[(1, 0)].start()
        near_first[4].wait_recv()
        near_core[(0, 2)].start()

    def near_forward_third():
        near_second[0].wait_recv()
        near_third[0].start()
        near_core[(-1, 3)].start()
        near_second[3].wait_recv()
        near_third[1].start()
        near_core[(1, 1)].start()
        near_second[1].wait_recv()
        near_core[(1, 3)].start()
        near_second[2].wait_recv()
        near_core[(-1, 1)].start()

    def near_finish():
        near_third[0].wait_recv()
        near_core[(-1, 2)].start()
        near_third[1].wait_recv()
        near_core[(1, 2)].start()
        for cp in near_core.values():
            cp.wait_recv()

    def stream(operators, total, right, dims, columns):
        def chunk(start, size):
            rows = operators[pl.ds(start, size), :]
            result = lax.dot_general(rows, right, dims, preferred_element_type=f32)
            if columns == 256:
                wide[0, pl.ds(start, size), :] = result[:, :TILE]
                wide[1, pl.ds(start, size), :] = result[:, TILE:]
            else:
                tall[pl.ds(start, size), :] = result

        def step(i, carry):
            chunk(pl.multiple_of(i * CHUNK, CHUNK), CHUNK)
            return carry

        whole = total // CHUNK
        lax.fori_loop(0, whole, step, 0)
        if total % CHUNK:
            chunk(whole * CHUNK, total % CHUNK)

    lane = lax.broadcasted_iota(jnp.int32, (COEF, TILE), 1)

    near_forward_second()
    for cp in leaf_first[:4]:
        cp.start()
    leaf_core[(0, 0)].start()

    cp_m2m.wait()
    stream(m2m, 8 * COEF, leaf[:, :COEF].astype(bf16), NT, 256)
    total = None
    for o in range(8):
        part = wide[o // 4, pl.ds(o, COEF, stride=8), :]
        part = jnp.where(lane // 32 == o % 4, part, 0.0)
        total = part if total is None else total + part
    total = total + pltpu.roll(total, 64, 1)
    total = total + pltpu.roll(total, 32, 1)
    near_forward_third()
    leaf_first[4].start()
    stream(m2m, 8 * COEF, total.astype(bf16), NN, 128)
    total = None
    for o in range(8):
        part = tall[pl.ds(o, COEF, stride=8), :]
        part = jnp.where(lane % 32 // 4 == o, part, 0.0)
        total = part if total is None else total + part
    for shift in (16, 8, 4):
        total = total + pltpu.roll(total, shift, 1)
    coarse = jnp.concatenate([total, jnp.zeros((512 - COEF, TILE), f32)], axis=0)
    coarse = jnp.transpose(coarse, (1, 0))
    for c in range(4):
        sc3[0:4, c, :] = coarse[0:4, c * TILE : (c + 1) * TILE]
    core_base, y_base, x_base = core * 256, y * 64, x * 16
    coarse_tab[pl.ds(core_base + y_base + x_base + z * 4, 4)] = sc3[0:4].astype(bf16)

    def coarse_copy(i, base, size, device):
        return pltpu.make_async_remote_copy(
            src_ref=coarse_tab.at[pl.ds(base, size)], dst_ref=coarse_tab.at[pl.ds(base, size)],
            send_sem=coarse_send.at[i], recv_sem=coarse_recv.at[i],
            device_id=device, device_id_type=MESH,
        )

    coarse_z = [
        coarse_copy(i, core_base + y_base + x_base + z * 4, 4, plane_device(0, 0, i + 1))
        for i in range(3)
    ]
    coarse_x = [
        coarse_copy(3 + i, core_base + y_base + x_base, 16, plane_device(0, i + 1, 0))
        for i in range(3)
    ]
    coarse_y = [
        coarse_copy(6 + i, core_base + y_base, 64, plane_device(i + 1, 0, 0)) for i in range(3)
    ]
    coarse_c = [coarse_copy(9, core_base, 256, near_device(0, 0, 1))]
    for cp in coarse_z:
        cp.start()

    def features(s, carry):
        px, py, pz = near_tab[s, 0], near_tab[s, 1], near_tab[s, 2]
        rows = [px, py, pz, px * px + py * py + pz * pz, jnp.ones_like(px)]
        rows += [near_tab[s, 3], near_tab[s, 4], jnp.zeros_like(px)]
        for r, value in enumerate(rows):
            feat[pl.ds(s * TILES, TILES), r, :] = value
        return carry


    def near_tile(u, carry):
        own = feat[own_slot * TILES + u]
        row = lax.broadcasted_iota(jnp.int32, (8, TILE), 0)
        left = jnp.where(row < 3, -2.0 * own, 0.0)
        left = jnp.where(row == 3, 1.0, left)
        left = jnp.where(row == 4, own[3:4, :], left)
        high, middle, low = split3(left)
        left = jnp.concatenate([high, middle, low, high, middle, high], axis=0)
        left = jnp.transpose(left, (1, 0)).astype(bf16)
        inverse = jnp.transpose(jnp.broadcast_to(own[5:6, :], (TILE, TILE)), (1, 0))
        count = near_count[u]

        def one(k):
            tile = near_tiles[u, k] - (box - 1) * (TILES * 8)
            tile = jnp.where(k < count, tile, 0)
            source = feat[tile]
            high, middle, low = split3(source)
            right = jnp.concatenate([high, high, high, middle, middle, low], axis=0).astype(bf16)
            square = lax.dot_general(left, right, NN, preferred_element_type=f32)
            square = jnp.maximum(square, 1e-9)
            weight = jnp.where(k < count, source[6:7, :], 0.0)
            scale = lax.rsqrt(inverse + source[5:6, :])
            reciprocal = lax.rsqrt(square)
            return lax.erf(square * reciprocal * scale) * (reciprocal * weight)

        total = jnp.zeros((TILE, TILE), f32)
        for k in range(NNEAR):
            total = total + one(k)
        near_acc[pl.ds(u, 1), :] = jnp.transpose(jnp.sum(total, axis=1, keepdims=True), (1, 0))
        return carry


    def steps_between(u):
        @pl.when(u == 1)
        def _():
            for cp in coarse_x:
                cp.wait_recv()
            for cp in coarse_y:
                cp.start()

        @pl.when(u == 3)
        def _():
            for i, share in enumerate([(-1, 3), (1, 3)]):
                leaf_second[i].wait_recv()
                leaf_third[i].start()
                leaf_core[share].start()
            leaf_first[2].wait_recv()
            leaf_core[(-1, 0)].start()
            leaf_first[3].wait_recv()
            leaf_core[(1, 0)].start()

        @pl.when(u == 4)
        def _():
            for cp in coarse_y:
                cp.wait_recv()
            coarse_c[0].start()

        @pl.when(u == 8)
        def _():
            for i, share in enumerate([(-1, 1), (1, 1)]):
                leaf_second[2 + i].wait_recv()
                leaf_third[2 + i].start()
                leaf_core[share].start()
            leaf_first[4].wait_recv()
            leaf_core[(0, 2)].start()

        @pl.when(u == 12)
        def _():
            leaf_third[0].wait_recv()
            leaf_third[2].wait_recv()
            leaf_core[(-1, 2)].start()
            leaf_third[1].wait_recv()
            leaf_third[3].wait_recv()
            leaf_core[(1, 2)].start()

    def tile_and_steps(u, carry):
        near_tile(u, carry)
        steps_between(u)
        return carry

    leaf_first[0].wait_recv()
    leaf_second[0].start()
    leaf_second[1].start()
    leaf_core[(0, 3)].start()
    leaf_first[1].wait_recv()
    leaf_second[2].start()
    leaf_second[3].start()
    leaf_core[(0, 1)].start()

    cp_m2l.wait()
    m2l[pl.ds(NCLASS * COEF, NCLASS * 7), :] = jnp.zeros((NCLASS * 7, COEF), bf16)
    into = lax.broadcasted_iota(jnp.int32, (256, 256), 0)
    outof = lax.broadcasted_iota(jnp.int32, (256, 256), 1)
    permute = (outof == into % 16 * NCLASS + into // 16).astype(f32).astype(bf16)

    def unmix_step(i, carry):
        for j in range(4):
            start = pl.multiple_of((i * 4 + j) * 16, 16)
            rows = m2l[pl.ds(pl.multiple_of(start * NCLASS, 256), 256), :]
            apart = lax.dot_general(permute, rows, NN, preferred_element_type=f32)
            apart = jnp.concatenate([apart, jnp.zeros((256, 512 - COEF), f32)], axis=1)
            apart = apart.astype(bf16)
            for k in range(NCLASS):
                wd[k, pl.ds(start, 16), :] = apart[k * 16 : (k + 1) * 16, :]
        return carry

    lax.fori_loop(0, 7, unmix_step, 0)

    cp_idx.wait()
    raw = idx_vmem[...]
    rel = jnp.clip(raw - (box - 1) * (8 * LEAF), 0, LEAF_ROWS - 1)
    row = (rel // LEAF) * LEAF + (rel % 8) * 32 + (rel // 8 % 8) * 4 + rel % LEAF // 64
    idx_vmem[...] = jnp.where(raw < 0, LEAF_ROWS, row)
    cp_smem = local(5, idx_vmem, idx)
    cp_smem.start()

    for cp in coarse_z:
        cp.wait_recv()
    for cp in coarse_x:
        cp.start()
    near_finish()
    lax.fori_loop(0, 24, features, 0)
    lax.fori_loop(0, TILES, tile_and_steps, 0)
    coarse_c[0].wait_recv()

    for k in range(NCLASS):
        for t in range(4):
            g = coarse_source[k, pair * 4 + t]
            home, member = g >> 5, (g >> 2) & 7
            place = (member & 1) * 256 + home * 16 + (member >> 1) * 4 + (g & 3)
            place = jnp.where(g < 0, COARSE_ROWS, place)
            gat[pl.ds((k * 4 + t) * 4, 4), :] = coarse_tab[place].astype(f32)
    picked = [gat[pl.ds(c, 64, stride=4), :] for c in range(4)]
    picked = jnp.concatenate(picked, axis=1)
    picked = jnp.concatenate([picked, picked], axis=0).astype(bf16)
    stream(m2l, NCLASS * COEF, picked[:, :COEF], NT, 128)
    total = None
    for k in range(NCLASS):
        part = tall[pl.ds(k, COEF, stride=NCLASS), :]
        part = jnp.where(lane % 64 // 4 == k, part, 0.0)
        total = part if total is None else total + part
    for shift in (32, 16, 8, 4):
        total = total + pltpu.roll(total, shift, 1)

    cp_l2l.wait()
    stream(l2l, 8 * COEF, total.astype(bf16), NN, 128)
    total = None
    for o in range(8):
        part = tall[pl.ds(o, COEF, stride=8), :]
        part = jnp.where(lane % 32 // 4 == o, part, 0.0)
        total = part if total is None else total + part
    stream(l2l, 8 * COEF, total.astype(bf16), NN, 128)
    acc[...] = jnp.zeros((448, LEAF), f32)
    for side in range(2):
        total = None
        for o in range(4):
            part = tall[pl.ds(side * 4 + o, COEF, stride=8), :]
            part = jnp.where(lane // 32 == o, part, 0.0)
            total = part if total is None else total + part
        acc[pl.ds(0, COEF), pl.ds(side * TILE, TILE)] = total

    cp_smem.wait()
    for cp in leaf_core.values():
        cp.wait_recv()

    def gather(k, into_ref):
        for start in range(0, LEAF, 16):
            values = []
            for j in range(start, start + 16):
                column = (j % 4) * 64 + (j % 32 // 4) * 8 + j // 32
                values.append(leaf_tab[idx[k, column]].astype(f32))
            for j in range(16):
                into_ref[pl.ds((start + j) * 4, 4), :] = values[j]

    def apply(k, from_ref):
        picked = [from_ref[pl.ds(c, LEAF, stride=4), :].astype(bf16) for c in range(4)]
        picked = jnp.concatenate(picked, axis=1)
        acc[...] += lax.dot_general(wd[k], picked, NT, preferred_element_type=f32)

    gather(0, gat)

    def leaf_class(i, carry):
        gather(2 * i + 1, gat_other)
        apply(2 * i, gat)
        gather(lax.rem(2 * i + 2, NCLASS), gat)
        apply(2 * i + 1, gat_other)
        return carry

    lax.fori_loop(0, NCLASS // 2, leaf_class, 0)

    locals_ = jnp.transpose(acc[...], (1, 0)).astype(bf16)[:, :COEF]
    for q in range(8):
        columns = mult[:, q * 256 : (q + 1) * 256]
        product = lax.dot_general(locals_, columns, NN, preferred_element_type=f32)
        for h in range(2):
            i = q * 2 + h
            hit = row_iota == rowidx[i : i + 1, :]
            far = jnp.where(hit, product[:, h * TILE : (h + 1) * TILE], 0.0)
            far = jnp.sum(far, axis=0, keepdims=True)
            out_ref[i : i + 1, :] = near_acc[i : i + 1, :] + far

    copies = near_first + near_second + near_third + list(near_core.values())
    copies += leaf_first + leaf_second + leaf_third + list(leaf_core.values())
    copies += coarse_z + coarse_x + coarse_y + coarse_c
    for cp in copies:
        cp.wait_send()


def body(
    multipoles, density, pair_centers, pair_exponent, box_of_pair, near_tiles, near_count,
    m2l_source, coarse_source, m2m_ops, l2l_ops, m2l_ops,
):
    def flat(operators):
        return jnp.transpose(operators, (1, 0, 2)).reshape(-1, COEF)

    grid = (TILES, TILE)
    smem = pl.BlockSpec(memory_space=pltpu.SMEM)
    vmem = pl.BlockSpec(memory_space=pltpu.VMEM)
    anywhere = pl.BlockSpec(memory_space=pl.ANY)
    dma = pltpu.SemaphoreType.DMA
    out = pl.pallas_call(
        kernel,
        out_shape=jax.ShapeDtypeStruct(grid, f32),
        in_specs=[smem, smem, smem, anywhere, vmem, vmem, vmem, vmem]
        + [anywhere, anywhere, anywhere, anywhere],
        out_specs=vmem,
        scratch_shapes=[
            pltpu.VMEM((COEF, 2048), bf16),
            pltpu.VMEM((8 * COEF, COEF), bf16),
            pltpu.VMEM((8 * COEF, COEF), bf16),
            pltpu.VMEM((NCLASS * 448, COEF), bf16),
            pltpu.VMEM((NCLASS, LEAF), jnp.int32),
            pltpu.SMEM((NCLASS, LEAF), jnp.int32),
            pltpu.VMEM((24, 5, TILES, TILE), f32),
            pltpu.VMEM((24 * TILES, 8, TILE), f32),
            pltpu.VMEM((LEAF_ROWS + ZERO_PAD, 4, TILE), bf16),
            pltpu.VMEM((COARSE_ROWS + ZERO_PAD, 4, TILE), bf16),
            pltpu.VMEM((LEAF, 4, TILE), f32),
            pltpu.VMEM((LEAF, 2048), bf16),
            pltpu.VMEM(grid, jnp.int32),
            pltpu.VMEM((2, 8 * COEF, TILE), f32),
            pltpu.VMEM((NCLASS * COEF, TILE), f32),
            pltpu.VMEM((NCLASS, 448, 512), bf16),
            pltpu.VMEM((1024, TILE), f32),
            pltpu.VMEM((1024, TILE), f32),
            pltpu.VMEM((448, LEAF), f32),
            pltpu.VMEM(grid, f32),
            dma((6,)),
            dma((23,)), dma((23,)), dma((25,)), dma((25,)), dma((10,)), dma((10,)),
        ],
        compiler_params=pltpu.CompilerParams(
            collective_id=0, has_side_effects=True, vmem_limit_bytes=60 * 1024 * 1024
        ),
    )(
        near_tiles, near_count, jnp.transpose(coarse_source), multipoles,
        density.reshape(grid), pair_centers, pair_exponent.reshape(grid),
        box_of_pair.reshape(grid), jnp.transpose(m2l_source),
        flat(m2m_ops), flat(l2l_ops), flat(m2l_ops),
    )
    return out.reshape(-1)


def solution(mesh):
    return jax.shard_map(
        body,
        mesh=mesh,
        in_specs=(
            P(None, ("box", "pair")),
            P(("box", "pair")),
            P(None, ("box", "pair")),
            P(("box", "pair")),
            P(("box", "pair")),
            P(("box", "pair"), None),
            P(("box", "pair")),
            P("box", None),
            P("box", None),
            P(),
            P(),
            P(),
        ),
        out_specs=P(("box", "pair")),
        check_vma=False,
    )
```

```python
import jax
import jax.numpy as jnp
from jax import lax
from jax.experimental import pallas as pl
from jax.experimental.pallas import tpu as pltpu
from jax.sharding import PartitionSpec as P

MESH = pl.DeviceIdType.MESH
NT = (((1,), (1,)), ((), ()))
NN = (((1,), (0,)), ((), ()))
TILE = 128
TILES = 16
NNEAR = 24
COEF = 441
LEAF = 256
NCLASS = 16
BOXES = 16
LEAF_ROWS = 24 * LEAF
COARSE_ROWS = 512
ZERO_PAD = 16
CHUNK = 1184
f32, bf16 = jnp.float32, jnp.bfloat16

HOPS = [(0, 1), (0, 3), (1, 0), (-1, 0), (0, 2)]
NEAR_SECOND = [((0, dz), (dx, 0)) for dz in (3, 1, 2) for dx in (1, -1)]
OWN = (0, 0)
FIRST = [(OWN, (0, 1), 0), (OWN, (0, 3), 1), (OWN, (1, 0), None), (OWN, (-1, 0), None)]
FIRST_B = [(OWN, (0, 1), 1), (OWN, (0, 3), 0), (OWN, (0, 2), None)]
SECOND = [((0, 3), (1, 0), 0), ((0, 3), (-1, 0), 0), ((0, 1), (1, 0), 1), ((0, 1), (-1, 0), 1)]
SECOND_B = [((0, 3), (1, 0), 1), ((0, 3), (-1, 0), 1), ((0, 1), (1, 0), 0), ((0, 1), (-1, 0), 0)]
THIRD = [((-1, 3), (0, 1), 0), ((1, 3), (0, 1), 0), ((-1, 1), (0, 3), 1), ((1, 1), (0, 3), 1)]
ALL_SHARES = [(dx, dz) for dx in (-1, 0, 1) for dz in range(4)]


def split3(values):
    high = values.astype(bf16).astype(f32)
    rest = values - high
    middle = rest.astype(bf16).astype(f32)
    return high, middle, rest - middle


def kernel(
    near_tiles, near_count, coarse_source, mult_hbm, dens_ref, cent_ref, expo_ref, box_ref,
    m2l_source, m2m_hbm, l2l_hbm, m2l_hbm, out_ref,
    mult, m2m, l2l, m2l, idx_vmem, idx, near_tab, feat, leaf_tab, coarse_tab, sc3, onehot, rowidx,
    wide, tall, wd, gat, gat_other, acc, near_acc, picked_ref,
    loc_sem, near_send, near_recv, leaf_send, leaf_recv, coarse_send, coarse_recv,
):
    box = lax.axis_index("box")
    pair = lax.axis_index("pair")
    y, x = box // 4, box % 4
    z, core = pair // 2, pair % 2

    def slot_of(dx, dz, which):
        return (dx + 1) * 8 + ((z + dz) % 4) * 2 + which

    def near_device(ndx, ndz, flip=0):
        other = core if not flip else 1 - core
        return ((box + ndx + BOXES) % BOXES, ((z + ndz) % 4) * 2 + other)

    def plane_device(dy, dx, dz):
        return (((y + dy) % 4) * 4 + (x + dx) % 4, ((z + dz) % 4) * 2 + core)

    def local(i, src, dst):
        return pltpu.make_async_copy(src, dst, loc_sem.at[i])

    own_cols = pl.ds(pl.multiple_of(pair * LEAF, LEAF), LEAF)
    cp_mult = local(0, mult_hbm, mult)
    cp_m2m = local(1, m2m_hbm, m2m)
    cp_m2l = local(2, m2l_hbm, m2l.at[pl.ds(0, NCLASS * COEF)])
    cp_l2l = local(3, l2l_hbm, l2l)
    cp_idx = local(4, m2l_source.at[:, own_cols], idx_vmem)
    cp_mult.start()
    cp_idx.start()
    cp_m2m.start()
    cp_m2l.start()
    cp_l2l.start()

    partners = [near_device(*hop) for hop in HOPS] + [near_device(0, 0, 1)]
    partners += [plane_device(0, d, 0) for d in (1, 2, 3)]
    partners += [plane_device(d, 0, 0) for d in (1, 2, 3)]
    barrier = pltpu.get_barrier_semaphore()
    for device in partners:
        pl.semaphore_signal(barrier, inc=1, device_id=device, device_id_type=MESH)

    own_slot = slot_of(0, 0, core)
    for c in range(3):
        for i in range(TILES):
            row = cent_ref[c : c + 1, i * TILE : (i + 1) * TILE] - 2.0
            near_tab[own_slot, c, i : i + 1, :] = row
    near_tab[own_slot, 3] = 1.0 / expo_ref[...]
    near_tab[own_slot, 4] = dens_ref[...]
    pl.semaphore_wait(barrier, len(partners))

    def near_ref(dx, dz, which):
        return near_tab.at[slot_of(dx, dz, which)]

    def leaf_ref(dx, dz, which, half=None):
        base, size = slot_of(dx, dz, which) * LEAF, LEAF
        if half is not None:
            base, size = base + half * (LEAF // 2), LEAF // 2
        return leaf_tab.at[pl.ds(base, size)]

    def near_copy(i, share, hop, flip=0):
        (dx, dz), (ndx, ndz) = share, hop
        return pltpu.make_async_remote_copy(
            src_ref=near_ref(dx, dz, core),
            dst_ref=near_tab.at[(dx - ndx + 1) * 8 + ((z + dz) % 4) * 2 + core],
            send_sem=near_send.at[i], recv_sem=near_recv.at[i],
            device_id=near_device(ndx, ndz, flip), device_id_type=MESH,
        )

    def leaf_copy(i, share, hop, half=None, flip=0):
        (dx, dz), (ndx, ndz) = share, hop
        return pltpu.make_async_remote_copy(
            src_ref=leaf_ref(dx, dz, core, half), dst_ref=leaf_ref(dx - ndx, dz, core, half),
            send_sem=leaf_send.at[i], recv_sem=leaf_recv.at[i],
            device_id=near_device(ndx, ndz, flip), device_id_type=MESH,
        )

    near_first = [near_copy(i, OWN, hop) for i, hop in enumerate(HOPS)]
    near_second = [near_copy(5 + i, *t) for i, t in enumerate(NEAR_SECOND)]
    near_core = {s: near_copy(11 + i, s, OWN, 1) for i, s in enumerate(ALL_SHARES)}
    leaf_first = [leaf_copy(i, *t) for i, t in enumerate(FIRST)]
    leaf_first_b = [leaf_copy(4 + i, *t) for i, t in enumerate(FIRST_B)]
    leaf_second = [leaf_copy(7 + i, *t) for i, t in enumerate(SECOND)]
    leaf_second_b = [leaf_copy(11 + i, *t) for i, t in enumerate(SECOND_B)]
    leaf_third = [leaf_copy(15 + i, *t) for i, t in enumerate(THIRD)]
    leaf_core = {s: leaf_copy(19 + i, s, OWN, None, 1) for i, s in enumerate(ALL_SHARES)}

    for cp in near_first:
        cp.start()
    near_core[(0, 0)].start()

    local_box = box_ref[...] - (box * (8 * LEAF) + pair * LEAF)
    rowidx[...] = (local_box % 8) * 32 + (local_box // 8 % 8) * 4 + local_box // 64
    row_iota = lax.broadcasted_iota(jnp.int32, (LEAF, TILE), 0)
    for i in range(TILES):
        weight = dens_ref[i : i + 1, :].astype(bf16).astype(f32)
        hit = row_iota == rowidx[i : i + 1, :]
        onehot[:, i * TILE : (i + 1) * TILE] = jnp.where(hit, weight, 0.0).astype(bf16)
    leaf_tab[pl.ds(LEAF_ROWS, ZERO_PAD)] = jnp.zeros((ZERO_PAD, 4, TILE), bf16)
    coarse_tab[pl.ds(COARSE_ROWS, ZERO_PAD)] = jnp.zeros((ZERO_PAD, 4, TILE), bf16)
    cp_mult.wait()
    leaf = lax.dot_general(onehot[...], mult[...], NT, preferred_element_type=f32)
    leaf = jnp.concatenate([leaf, jnp.zeros((LEAF, 512 - COEF), f32)], axis=1)
    for c in range(4):
        sc3[:, c, :] = leaf[:, c * TILE : (c + 1) * TILE]
    leaf_tab[pl.ds(own_slot * LEAF, LEAF)] = sc3[...].astype(bf16)

    def product(operators, start, size, right, dims):
        rows = operators[pl.ds(start, size), :]
        result = lax.dot_general(rows, right, dims, preferred_element_type=f32)
        if result.shape[1] == 256:
            wide[0, pl.ds(start, size), :] = result[:, :TILE]
            wide[1, pl.ds(start, size), :] = result[:, TILE:]
        else:
            tall[pl.ds(start, size), :] = result

    def stream(operators, total, right, dims):
        def step(i, carry):
            product(operators, pl.multiple_of(i * CHUNK, CHUNK), CHUNK, right, dims)
            return carry

        whole = total // CHUNK
        lax.fori_loop(0, whole, step, 0)
        if total % CHUNK:
            product(operators, whole * CHUNK, total % CHUNK, right, dims)

    lane = lax.broadcasted_iota(jnp.int32, (COEF, TILE), 1)

    leaf_first[0].start()
    leaf_first[1].start()
    leaf_core[(0, 0)].start()

    cp_m2m.wait()
    stream(m2m, 8 * COEF, leaf[:, :COEF].astype(bf16), NT)
    total = None
    for o in range(8):
        part = wide[o // 4, pl.ds(o, COEF, stride=8), :]
        part = jnp.where(lane // 32 == o % 4, part, 0.0)
        total = part if total is None else total + part
    total = total + pltpu.roll(total, 64, 1)
    total = total + pltpu.roll(total, 32, 1)
    for j, dz in enumerate((3, 1, 2)):
        near_first[(0, 1, 4)[j]].wait_recv()
        near_second[2 * j].start()
        near_second[2 * j + 1].start()
        near_core[(0, dz)].start()
    leaf_first[2].start()
    leaf_first[3].start()
    stream(m2m, 8 * COEF, total.astype(bf16), NN)
    total = None
    for o in range(8):
        part = tall[pl.ds(o, COEF, stride=8), :]
        part = jnp.where(lane % 32 // 4 == o, part, 0.0)
        total = part if total is None else total + part
    for shift in (16, 8, 4):
        total = total + pltpu.roll(total, shift, 1)
    coarse = jnp.concatenate([total, jnp.zeros((512 - COEF, TILE), f32)], axis=0)
    coarse = jnp.transpose(coarse, (1, 0))
    for c in range(4):
        sc3[0:4, c, :] = coarse[0:4, c * TILE : (c + 1) * TILE]
    core_base, y_base, x_base = core * 256, y * 64, x * 16
    coarse_tab[pl.ds(core_base + y_base + x_base + z * 4, 4)] = sc3[0:4].astype(bf16)

    def coarse_copy(i, base, size, device):
        return pltpu.make_async_remote_copy(
            src_ref=coarse_tab.at[pl.ds(base, size)], dst_ref=coarse_tab.at[pl.ds(base, size)],
            send_sem=coarse_send.at[i], recv_sem=coarse_recv.at[i],
            device_id=device, device_id_type=MESH,
        )

    coarse_z = [
        coarse_copy(i, core_base + y_base + x_base + z * 4, 4, plane_device(0, 0, i + 1))
        for i in range(3)
    ]
    coarse_x = [
        coarse_copy(3 + i, core_base + y_base + x_base, 16, plane_device(0, i + 1, 0))
        for i in range(3)
    ]
    coarse_y = [
        coarse_copy(6 + i, core_base + y_base, 64, plane_device(i + 1, 0, 0)) for i in range(3)
    ]
    coarse_c = [coarse_copy(9, core_base, 256, near_device(0, 0, 1))]
    for cp in coarse_z:
        cp.start()
    for cp in leaf_first_b:
        cp.start()
    near_first[2].wait_recv()
    near_core[(-1, 0)].start()
    near_first[3].wait_recv()
    near_core[(1, 0)].start()

    def features(s, carry):
        px, py, pz = near_tab[s, 0], near_tab[s, 1], near_tab[s, 2]
        rows = [px, py, pz, px * px + py * py + pz * pz, jnp.ones_like(px)]
        rows += [near_tab[s, 3], near_tab[s, 4], jnp.zeros_like(px)]
        for r, value in enumerate(rows):
            feat[pl.ds(s * TILES, TILES), r, :] = value
        return carry


    def near_tile(u, carry):
        own = feat[own_slot * TILES + u]
        row = lax.broadcasted_iota(jnp.int32, (8, TILE), 0)
        left = jnp.where(row < 3, -2.0 * own, 0.0)
        left = jnp.where(row == 3, 1.0, left)
        left = jnp.where(row == 4, own[3:4, :], left)
        high, middle, low = split3(left)
        left = jnp.concatenate([high, middle, low, high, middle, high], axis=0)
        left = jnp.transpose(left, (1, 0)).astype(bf16)
        inverse = jnp.transpose(jnp.broadcast_to(own[5:6, :], (TILE, TILE)), (1, 0))
        count = near_count[u]

        def one(k):
            tile = near_tiles[u, k] - (box - 1) * (TILES * 8)
            tile = jnp.where(k < count, tile, 0)
            source = feat[tile]
            high, middle, low = split3(source)
            right = jnp.concatenate([high, high, high, middle, middle, low], axis=0).astype(bf16)
            square = lax.dot_general(left, right, NN, preferred_element_type=f32)
            square = jnp.maximum(square, 1e-9)
            weight = jnp.where(k < count, source[6:7, :], 0.0)
            scale = lax.rsqrt(inverse + source[5:6, :])
            reciprocal = lax.rsqrt(square)
            return lax.erf(square * reciprocal * scale) * (reciprocal * weight)

        total = jnp.zeros((TILE, TILE), f32)
        for k in range(NNEAR):
            total = total + one(k)
        near_acc[pl.ds(u, 1), :] = jnp.transpose(jnp.sum(total, axis=1, keepdims=True), (1, 0))
        return carry


    def steps_between(u):
        @pl.when(u == 1)
        def _():
            leaf_first_b[0].wait_recv()
            leaf_second_b[0].start()
            leaf_second_b[1].start()
            leaf_core[(0, 3)].start()
            leaf_first_b[1].wait_recv()
            leaf_second_b[2].start()
            leaf_second_b[3].start()
            leaf_core[(0, 1)].start()
            leaf_first[2].wait_recv()
            leaf_core[(-1, 0)].start()
            leaf_first[3].wait_recv()
            leaf_core[(1, 0)].start()

        @pl.when(u == 4)
        def _():
            for cp in coarse_x:
                cp.wait_recv()
            for cp in coarse_y:
                cp.start()

        @pl.when(u == 6)
        def _():
            for cp in coarse_y:
                cp.wait_recv()
            coarse_c[0].start()

        @pl.when(u == 9)
        def _():
            for i in range(4):
                leaf_second[i].wait_recv()
                leaf_third[i].start()
            leaf_first_b[2].wait_recv()
            leaf_core[(0, 2)].start()

        @pl.when(u == 13)
        def _():
            for i, share in enumerate([(-1, 3), (1, 3), (-1, 1), (1, 1)]):
                leaf_second_b[i].wait_recv()
                leaf_core[share].start()

    def tile_and_steps(u, carry):
        near_tile(u, carry)
        steps_between(u)
        return carry

    cp_m2l.wait()
    m2l[pl.ds(NCLASS * COEF, NCLASS * 7), :] = jnp.zeros((NCLASS * 7, COEF), bf16)
    into = lax.broadcasted_iota(jnp.int32, (256, 256), 0)
    outof = lax.broadcasted_iota(jnp.int32, (256, 256), 1)
    permute = (outof == into % 16 * NCLASS + into // 16).astype(f32).astype(bf16)

    def unmix_step(i, carry):
        for j in range(4):
            start = pl.multiple_of((i * 4 + j) * 16, 16)
            rows = m2l[pl.ds(pl.multiple_of(start * NCLASS, 256), 256), :]
            apart = lax.dot_general(permute, rows, NN, preferred_element_type=f32)
            apart = jnp.concatenate([apart, jnp.zeros((256, 512 - COEF), f32)], axis=1)
            apart = apart.astype(bf16)
            for k in range(NCLASS):
                wd[k, pl.ds(start, 16), :] = apart[k * 16 : (k + 1) * 16, :]
        return carry

    lax.fori_loop(0, 7, unmix_step, 0)

    cp_idx.wait()
    raw = idx_vmem[...]
    rel = jnp.clip(raw - (box - 1) * (8 * LEAF), 0, LEAF_ROWS - 1)
    row = (rel // LEAF) * LEAF + (rel % 8) * 32 + (rel // 8 % 8) * 4 + rel % LEAF // 64
    idx_vmem[...] = jnp.where(raw < 0, LEAF_ROWS, row)
    cp_smem = local(5, idx_vmem, idx)
    cp_smem.start()

    for cp in coarse_z:
        cp.wait_recv()
    for cp in coarse_x:
        cp.start()
    leaf_first[0].wait_recv()
    leaf_second[0].start()
    leaf_second[1].start()
    leaf_first[1].wait_recv()
    leaf_second[2].start()
    leaf_second[3].start()
    for ((_, dz), (dx, _)), cp in zip(NEAR_SECOND, near_second):
        cp.wait_recv()
        near_core[(-dx, dz)].start()
    for cp in near_core.values():
        cp.wait_recv()
    lax.fori_loop(0, 24, features, 0)
    lax.fori_loop(0, 8, tile_and_steps, 0)
    coarse_c[0].wait_recv()

    for k in range(NCLASS):
        for t in range(4):
            g = coarse_source[k, pair * 4 + t]
            home, member = g >> 5, (g >> 2) & 7
            place = (member & 1) * 256 + home * 16 + (member >> 1) * 4 + (g & 3)
            place = jnp.where(g < 0, COARSE_ROWS, place)
            gat[pl.ds((k * 4 + t) * 4, 4), :] = coarse_tab[place].astype(f32)
    picked = [gat[pl.ds(c, 64, stride=4), :] for c in range(4)]
    picked = jnp.concatenate(picked, axis=1)
    picked = jnp.concatenate([picked, picked], axis=0).astype(bf16)
    picked_ref[...] = picked

    def tile_and_m2l(i, carry):
        start = jnp.minimum(i * CHUNK, NCLASS * COEF - CHUNK)
        start = pl.multiple_of(start, 16)
        product(m2l, start, CHUNK, picked_ref[:, :COEF], NT)
        return tile_and_steps(i + 8, carry)

    lax.fori_loop(0, 6, tile_and_m2l, 0)
    total = None
    for k in range(NCLASS):
        part = tall[pl.ds(k, COEF, stride=NCLASS), :]
        part = jnp.where(lane % 64 // 4 == k, part, 0.0)
        total = part if total is None else total + part
    for shift in (32, 16, 8, 4):
        total = total + pltpu.roll(total, shift, 1)

    cp_l2l.wait()
    right = total.astype(bf16)
    for i, (start, size) in enumerate([(0, 1776), (1776, 8 * COEF - 1776)]):
        product(l2l, start, size, right, NN)
    near_tile(14, 0)
    total = None
    for o in range(8):
        part = tall[pl.ds(o, COEF, stride=8), :]
        part = jnp.where(lane % 32 // 4 == o, part, 0.0)
        total = part if total is None else total + part
    right = total.astype(bf16)
    for i, (start, size) in enumerate([(0, 1776), (1776, 8 * COEF - 1776)]):
        product(l2l, start, size, right, NN)
    near_tile(15, 0)
    leaf_third[0].wait_recv()
    leaf_third[2].wait_recv()
    leaf_core[(-1, 2)].start()
    leaf_third[1].wait_recv()
    leaf_third[3].wait_recv()
    leaf_core[(1, 2)].start()
    acc[...] = jnp.zeros((448, LEAF), f32)
    for side in range(2):
        total = None
        for o in range(4):
            part = tall[pl.ds(side * 4 + o, COEF, stride=8), :]
            part = jnp.where(lane // 32 == o, part, 0.0)
            total = part if total is None else total + part
        acc[pl.ds(0, COEF), pl.ds(side * TILE, TILE)] = total

    cp_smem.wait()
    for cp in leaf_core.values():
        cp.wait_recv()

    def gather(k, into_ref):
        for start in range(0, LEAF, 16):
            values = []
            for j in range(start, start + 16):
                column = (j % 4) * 64 + (j % 32 // 4) * 8 + j // 32
                values.append(leaf_tab[idx[k, column]].astype(f32))
            for j in range(16):
                into_ref[pl.ds((start + j) * 4, 4), :] = values[j]

    def apply(k, from_ref):
        picked = [from_ref[pl.ds(c, LEAF, stride=4), :].astype(bf16) for c in range(4)]
        picked = jnp.concatenate(picked, axis=1)
        acc[...] += lax.dot_general(wd[k], picked, NT, preferred_element_type=f32)

    gather(0, gat)

    def leaf_class(i, carry):
        gather(2 * i + 1, gat_other)
        apply(2 * i, gat)
        gather(lax.rem(2 * i + 2, NCLASS), gat)
        apply(2 * i + 1, gat_other)
        return carry

    lax.fori_loop(0, NCLASS // 2, leaf_class, 0)

    locals_ = jnp.transpose(acc[...], (1, 0)).astype(bf16)[:, :COEF]
    for q in range(8):
        columns = mult[:, q * 256 : (q + 1) * 256]
        product = lax.dot_general(locals_, columns, NN, preferred_element_type=f32)
        for h in range(2):
            i = q * 2 + h
            hit = row_iota == rowidx[i : i + 1, :]
            far = jnp.where(hit, product[:, h * TILE : (h + 1) * TILE], 0.0)
            far = jnp.sum(far, axis=0, keepdims=True)
            out_ref[i : i + 1, :] = near_acc[i : i + 1, :] + far

    copies = near_first + near_second + list(near_core.values())
    copies += leaf_first + leaf_first_b + leaf_second + leaf_second_b + leaf_third
    copies += list(leaf_core.values())
    copies += coarse_z + coarse_x + coarse_y + coarse_c
    for cp in copies:
        cp.wait_send()


def body(
    multipoles, density, pair_centers, pair_exponent, box_of_pair, near_tiles, near_count,
    m2l_source, coarse_source, m2m_ops, l2l_ops, m2l_ops,
):
    def flat(operators):
        return jnp.transpose(operators, (1, 0, 2)).reshape(-1, COEF)

    grid = (TILES, TILE)
    smem = pl.BlockSpec(memory_space=pltpu.SMEM)
    vmem = pl.BlockSpec(memory_space=pltpu.VMEM)
    anywhere = pl.BlockSpec(memory_space=pl.ANY)
    dma = pltpu.SemaphoreType.DMA
    out = pl.pallas_call(
        kernel,
        out_shape=jax.ShapeDtypeStruct(grid, f32),
        in_specs=[smem, smem, smem, anywhere, vmem, vmem, vmem, vmem]
        + [anywhere, anywhere, anywhere, anywhere],
        out_specs=vmem,
        scratch_shapes=[
            pltpu.VMEM((COEF, 2048), bf16),
            pltpu.VMEM((8 * COEF, COEF), bf16),
            pltpu.VMEM((8 * COEF, COEF), bf16),
            pltpu.VMEM((NCLASS * 448, COEF), bf16),
            pltpu.VMEM((NCLASS, LEAF), jnp.int32),
            pltpu.SMEM((NCLASS, LEAF), jnp.int32),
            pltpu.VMEM((24, 5, TILES, TILE), f32),
            pltpu.VMEM((24 * TILES, 8, TILE), f32),
            pltpu.VMEM((LEAF_ROWS + ZERO_PAD, 4, TILE), bf16),
            pltpu.VMEM((COARSE_ROWS + ZERO_PAD, 4, TILE), bf16),
            pltpu.VMEM((LEAF, 4, TILE), f32),
            pltpu.VMEM((LEAF, 2048), bf16),
            pltpu.VMEM(grid, jnp.int32),
            pltpu.VMEM((2, 8 * COEF, TILE), f32),
            pltpu.VMEM((NCLASS * COEF, TILE), f32),
            pltpu.VMEM((NCLASS, 448, 512), bf16),
            pltpu.VMEM((1024, TILE), f32),
            pltpu.VMEM((1024, TILE), f32),
            pltpu.VMEM((448, LEAF), f32),
            pltpu.VMEM(grid, f32),
            pltpu.VMEM((TILE, 512), bf16),
            dma((6,)),
            dma((23,)), dma((23,)), dma((31,)), dma((31,)), dma((10,)), dma((10,)),
        ],
        compiler_params=pltpu.CompilerParams(
            collective_id=0, has_side_effects=True, vmem_limit_bytes=60 * 1024 * 1024
        ),
    )(
        near_tiles, near_count, jnp.transpose(coarse_source), multipoles,
        density.reshape(grid), pair_centers, pair_exponent.reshape(grid),
        box_of_pair.reshape(grid), jnp.transpose(m2l_source),
        flat(m2m_ops), flat(l2l_ops), flat(m2l_ops),
    )
    return out.reshape(-1)


def solution(mesh):
    return jax.shard_map(
        body,
        mesh=mesh,
        in_specs=(
            P(None, ("box", "pair")),
            P(("box", "pair")),
            P(None, ("box", "pair")),
            P(("box", "pair")),
            P(("box", "pair")),
            P(("box", "pair"), None),
            P(("box", "pair")),
            P("box", None),
            P("box", None),
            P(),
            P(),
            P(),
        ),
        out_specs=P(("box", "pair")),
        check_vma=False,
    )
```

```python
import jax
import jax.numpy as jnp
from jax import lax
from jax.experimental import pallas as pl
from jax.experimental.pallas import tpu as pltpu
from jax.sharding import PartitionSpec as P

MESH = pl.DeviceIdType.MESH
NT = (((1,), (1,)), ((), ()))
NN = (((1,), (0,)), ((), ()))
TILE = 128
TILES = 16
NNEAR = 24
COEF = 441
LEAF = 256
NCLASS = 16
BOXES = 16
LEAF_ROWS = 24 * LEAF
COARSE_ROWS = 512
ZERO_PAD = 16
CHUNK = 1184
f32, bf16 = jnp.float32, jnp.bfloat16

HOPS = [(0, 1), (0, 3), (1, 0), (-1, 0), (0, 2)]
NEAR_SECOND = [((0, dz), (dx, 0)) for dz in (3, 1, 2) for dx in (1, -1)]
OWN = (0, 0)
FIRST = [(OWN, (0, 1), 0), (OWN, (0, 3), 1), (OWN, (1, 0), 0), (OWN, (-1, 0), 0)]
FIRST_B = [(OWN, (0, 1), 1), (OWN, (0, 3), 0), (OWN, (0, 2), None)]
FIRST_B += [(OWN, (1, 0), 1), (OWN, (-1, 0), 1)]
SECOND = [((0, 3), (1, 0), 0), ((0, 3), (-1, 0), 0), ((0, 1), (1, 0), 1), ((0, 1), (-1, 0), 1)]
SECOND_B = [((0, 3), (1, 0), 1), ((0, 3), (-1, 0), 1), ((0, 1), (1, 0), 0), ((0, 1), (-1, 0), 0)]
THIRD = [((-1, 3), (0, 1), 0), ((1, 3), (0, 1), 0), ((-1, 1), (0, 3), 1), ((1, 1), (0, 3), 1)]
ALL_SHARES = [(dx, dz) for dx in (-1, 0, 1) for dz in range(4)]


def split3(values):
    high = values.astype(bf16).astype(f32)
    rest = values - high
    middle = rest.astype(bf16).astype(f32)
    return high, middle, rest - middle


def kernel(
    near_tiles, near_count, coarse_source, mult_hbm, dens_ref, cent_ref, expo_ref, box_ref,
    m2l_source, m2m_hbm, l2l_hbm, m2l_hbm, out_ref,
    mult, m2m, l2l, m2l, idx_vmem, idx, near_tab, feat, leaf_tab, coarse_tab, sc3, onehot, rowidx,
    wide, tall, wd, gat, gat_other, acc, near_acc, picked_ref,
    loc_sem, near_send, near_recv, leaf_send, leaf_recv, coarse_send, coarse_recv,
):
    box = lax.axis_index("box")
    pair = lax.axis_index("pair")
    y, x = box // 4, box % 4
    z, core = pair // 2, pair % 2

    def slot_of(dx, dz, which):
        return (dx + 1) * 8 + ((z + dz) % 4) * 2 + which

    def near_device(ndx, ndz, flip=0):
        other = core if not flip else 1 - core
        return ((box + ndx + BOXES) % BOXES, ((z + ndz) % 4) * 2 + other)

    def plane_device(dy, dx, dz):
        return (((y + dy) % 4) * 4 + (x + dx) % 4, ((z + dz) % 4) * 2 + core)

    def local(i, src, dst):
        return pltpu.make_async_copy(src, dst, loc_sem.at[i])

    own_cols = pl.ds(pl.multiple_of(pair * LEAF, LEAF), LEAF)
    cp_mult = local(0, mult_hbm, mult)
    cp_m2m = local(1, m2m_hbm, m2m)
    cp_m2l = local(2, m2l_hbm, m2l.at[pl.ds(0, NCLASS * COEF)])
    cp_l2l = local(3, l2l_hbm, l2l)
    cp_idx = local(4, m2l_source.at[:, own_cols], idx_vmem)
    cp_mult.start()
    cp_idx.start()
    cp_m2m.start()
    cp_m2l.start()
    cp_l2l.start()

    partners = [near_device(*hop) for hop in HOPS] + [near_device(0, 0, 1)]
    partners += [plane_device(0, d, 0) for d in (1, 2, 3)]
    partners += [plane_device(d, 0, 0) for d in (1, 2, 3)]
    barrier = pltpu.get_barrier_semaphore()
    for device in partners:
        pl.semaphore_signal(barrier, inc=1, device_id=device, device_id_type=MESH)

    own_slot = slot_of(0, 0, core)
    for c in range(3):
        for i in range(TILES):
            row = cent_ref[c : c + 1, i * TILE : (i + 1) * TILE] - 2.0
            near_tab[own_slot, c, i : i + 1, :] = row
    near_tab[own_slot, 3] = 1.0 / expo_ref[...]
    near_tab[own_slot, 4] = dens_ref[...]
    pl.semaphore_wait(barrier, len(partners))

    def near_ref(dx, dz, which):
        return near_tab.at[slot_of(dx, dz, which)]

    def leaf_ref(dx, dz, which, half=None):
        base, size = slot_of(dx, dz, which) * LEAF, LEAF
        if half is not None:
            base, size = base + half * (LEAF // 2), LEAF // 2
        return leaf_tab.at[pl.ds(base, size)]

    def near_copy(i, share, hop, flip=0):
        (dx, dz), (ndx, ndz) = share, hop
        return pltpu.make_async_remote_copy(
            src_ref=near_ref(dx, dz, core),
            dst_ref=near_tab.at[(dx - ndx + 1) * 8 + ((z + dz) % 4) * 2 + core],
            send_sem=near_send.at[i], recv_sem=near_recv.at[i],
            device_id=near_device(ndx, ndz, flip), device_id_type=MESH,
        )

    def leaf_copy(i, share, hop, half=None, flip=0):
        (dx, dz), (ndx, ndz) = share, hop
        return pltpu.make_async_remote_copy(
            src_ref=leaf_ref(dx, dz, core, half), dst_ref=leaf_ref(dx - ndx, dz, core, half),
            send_sem=leaf_send.at[i], recv_sem=leaf_recv.at[i],
            device_id=near_device(ndx, ndz, flip), device_id_type=MESH,
        )

    near_first = [near_copy(i, OWN, hop) for i, hop in enumerate(HOPS)]
    near_second = [near_copy(5 + i, *t) for i, t in enumerate(NEAR_SECOND)]
    near_core = {s: near_copy(11 + i, s, OWN, 1) for i, s in enumerate(ALL_SHARES)}
    leaf_first = [leaf_copy(i, *t) for i, t in enumerate(FIRST)]
    leaf_first_b = [leaf_copy(4 + i, *t) for i, t in enumerate(FIRST_B)]
    leaf_second = [leaf_copy(9 + i, *t) for i, t in enumerate(SECOND)]
    leaf_second_b = [leaf_copy(13 + i, *t) for i, t in enumerate(SECOND_B)]
    leaf_third = [leaf_copy(17 + i, *t) for i, t in enumerate(THIRD)]
    leaf_core = {s: leaf_copy(21 + i, s, OWN, None, 1) for i, s in enumerate(ALL_SHARES)}

    for cp in near_first:
        cp.start()
    near_core[(0, 0)].start()

    local_box = box_ref[...] - (box * (8 * LEAF) + pair * LEAF)
    rowidx[...] = (local_box % 8) * 32 + (local_box // 8 % 8) * 4 + local_box // 64
    row_iota = lax.broadcasted_iota(jnp.int32, (LEAF, TILE), 0)
    for i in range(TILES):
        weight = dens_ref[i : i + 1, :].astype(bf16).astype(f32)
        hit = row_iota == rowidx[i : i + 1, :]
        onehot[:, i * TILE : (i + 1) * TILE] = jnp.where(hit, weight, 0.0).astype(bf16)
    leaf_tab[pl.ds(LEAF_ROWS, ZERO_PAD)] = jnp.zeros((ZERO_PAD, 4, TILE), bf16)
    coarse_tab[pl.ds(COARSE_ROWS, ZERO_PAD)] = jnp.zeros((ZERO_PAD, 4, TILE), bf16)
    cp_mult.wait()
    leaf = lax.dot_general(onehot[...], mult[...], NT, preferred_element_type=f32)
    leaf = jnp.concatenate([leaf, jnp.zeros((LEAF, 512 - COEF), f32)], axis=1)
    for c in range(4):
        sc3[:, c, :] = leaf[:, c * TILE : (c + 1) * TILE]
    leaf_tab[pl.ds(own_slot * LEAF, LEAF)] = sc3[...].astype(bf16)

    def product(operators, start, size, right, dims):
        rows = operators[pl.ds(start, size), :]
        result = lax.dot_general(rows, right, dims, preferred_element_type=f32)
        if result.shape[1] == 256:
            wide[0, pl.ds(start, size), :] = result[:, :TILE]
            wide[1, pl.ds(start, size), :] = result[:, TILE:]
        else:
            tall[pl.ds(start, size), :] = result

    def stream(operators, total, right, dims):
        def step(i, carry):
            product(operators, pl.multiple_of(i * CHUNK, CHUNK), CHUNK, right, dims)
            return carry

        whole = total // CHUNK
        lax.fori_loop(0, whole, step, 0)
        if total % CHUNK:
            product(operators, whole * CHUNK, total % CHUNK, right, dims)

    lane = lax.broadcasted_iota(jnp.int32, (COEF, TILE), 1)

    leaf_first[0].start()
    leaf_first[1].start()
    leaf_core[(0, 0)].start()

    cp_m2m.wait()
    stream(m2m, 8 * COEF, leaf[:, :COEF].astype(bf16), NT)
    total = None
    for o in range(8):
        part = wide[o // 4, pl.ds(o, COEF, stride=8), :]
        part = jnp.where(lane // 32 == o % 4, part, 0.0)
        total = part if total is None else total + part
    total = total + pltpu.roll(total, 64, 1)
    total = total + pltpu.roll(total, 32, 1)
    for j, dz in enumerate((3, 1, 2)):
        near_first[(0, 1, 4)[j]].wait_recv()
        near_second[2 * j].start()
        near_second[2 * j + 1].start()
        near_core[(0, dz)].start()
    leaf_first[2].start()
    leaf_first[3].start()
    stream(m2m, 8 * COEF, total.astype(bf16), NN)
    total = None
    for o in range(8):
        part = tall[pl.ds(o, COEF, stride=8), :]
        part = jnp.where(lane % 32 // 4 == o, part, 0.0)
        total = part if total is None else total + part
    for shift in (16, 8, 4):
        total = total + pltpu.roll(total, shift, 1)
    coarse = jnp.concatenate([total, jnp.zeros((512 - COEF, TILE), f32)], axis=0)
    coarse = jnp.transpose(coarse, (1, 0))
    for c in range(4):
        sc3[0:4, c, :] = coarse[0:4, c * TILE : (c + 1) * TILE]
    core_base, y_base, x_base = core * 256, y * 64, x * 16
    coarse_tab[pl.ds(core_base + y_base + x_base + z * 4, 4)] = sc3[0:4].astype(bf16)

    def coarse_copy(i, base, size, device):
        return pltpu.make_async_remote_copy(
            src_ref=coarse_tab.at[pl.ds(base, size)], dst_ref=coarse_tab.at[pl.ds(base, size)],
            send_sem=coarse_send.at[i], recv_sem=coarse_recv.at[i],
            device_id=device, device_id_type=MESH,
        )

    coarse_z = [
        coarse_copy(i, core_base + y_base + x_base + z * 4, 4, plane_device(0, 0, i + 1))
        for i in range(3)
    ]
    coarse_x = [
        coarse_copy(3 + i, core_base + y_base + x_base, 16, plane_device(0, i + 1, 0))
        for i in range(3)
    ]
    coarse_y = [
        coarse_copy(6 + i, core_base + y_base, 64, plane_device(i + 1, 0, 0)) for i in range(3)
    ]
    coarse_c = [coarse_copy(9, core_base, 256, near_device(0, 0, 1))]
    for cp in coarse_z:
        cp.start()
    leaf_first_b[0].start()
    leaf_first_b[1].start()
    near_first[2].wait_recv()
    near_core[(-1, 0)].start()
    near_first[3].wait_recv()
    near_core[(1, 0)].start()

    def features(s, carry):
        px, py, pz = near_tab[s, 0], near_tab[s, 1], near_tab[s, 2]
        rows = [px, py, pz, px * px + py * py + pz * pz, jnp.ones_like(px)]
        rows += [near_tab[s, 3], near_tab[s, 4], jnp.zeros_like(px)]
        for r, value in enumerate(rows):
            feat[pl.ds(s * TILES, TILES), r, :] = value
        return carry


    def near_tile(u, carry):
        own = feat[own_slot * TILES + u]
        row = lax.broadcasted_iota(jnp.int32, (8, TILE), 0)
        left = jnp.where(row < 3, -2.0 * own, 0.0)
        left = jnp.where(row == 3, 1.0, left)
        left = jnp.where(row == 4, own[3:4, :], left)
        high, middle, low = split3(left)
        left = jnp.concatenate([high, middle, low, high, middle, high], axis=0)
        left = jnp.transpose(left, (1, 0)).astype(bf16)
        inverse = jnp.transpose(jnp.broadcast_to(own[5:6, :], (TILE, TILE)), (1, 0))
        count = near_count[u]

        def one(k):
            tile = near_tiles[u, k] - (box - 1) * (TILES * 8)
            tile = jnp.where(k < count, tile, 0)
            source = feat[tile]
            high, middle, low = split3(source)
            right = jnp.concatenate([high, high, high, middle, middle, low], axis=0).astype(bf16)
            square = lax.dot_general(left, right, NN, preferred_element_type=f32)
            square = jnp.maximum(square, 1e-9)
            weight = jnp.where(k < count, source[6:7, :], 0.0)
            scale = lax.rsqrt(inverse + source[5:6, :])
            reciprocal = lax.rsqrt(square)
            return lax.erf(square * reciprocal * scale) * (reciprocal * weight)

        total = jnp.zeros((TILE, TILE), f32)
        for k in range(NNEAR):
            total = total + one(k)
        near_acc[pl.ds(u, 1), :] = jnp.transpose(jnp.sum(total, axis=1, keepdims=True), (1, 0))
        return carry


    def steps_between(u):
        @pl.when(u == 3)
        def _():
            leaf_first_b[0].wait_recv()
            leaf_second_b[0].start()
            leaf_second_b[1].start()
            leaf_core[(0, 3)].start()
            leaf_first_b[1].wait_recv()
            leaf_second_b[2].start()
            leaf_second_b[3].start()
            leaf_core[(0, 1)].start()

        @pl.when(u == 4)
        def _():
            for cp in coarse_x:
                cp.wait_recv()
            for cp in coarse_y:
                cp.start()

        @pl.when(u == 7)
        def _():
            for cp in coarse_y:
                cp.wait_recv()
            coarse_c[0].start()

        @pl.when(u == 11)
        def _():
            for i, dx in enumerate((-1, 1)):
                leaf_first[2 + i].wait_recv()
                leaf_first_b[3 + i].wait_recv()
                leaf_core[(dx, 0)].start()
            for i in range(4):
                leaf_second[i].wait_recv()
                leaf_third[i].start()
            leaf_first_b[2].wait_recv()
            leaf_core[(0, 2)].start()

    def tile_and_steps(u, carry):
        near_tile(u, carry)
        steps_between(u)
        return carry

    cp_m2l.wait()
    m2l[pl.ds(NCLASS * COEF, NCLASS * 7), :] = jnp.zeros((NCLASS * 7, COEF), bf16)
    into = lax.broadcasted_iota(jnp.int32, (256, 256), 0)
    outof = lax.broadcasted_iota(jnp.int32, (256, 256), 1)
    permute = (outof == into % 16 * NCLASS + into // 16).astype(f32).astype(bf16)

    def unmix_step(i, carry):
        for j in range(4):
            start = pl.multiple_of((i * 4 + j) * 16, 16)
            rows = m2l[pl.ds(pl.multiple_of(start * NCLASS, 256), 256), :]
            apart = lax.dot_general(permute, rows, NN, preferred_element_type=f32)
            apart = jnp.concatenate([apart, jnp.zeros((256, 512 - COEF), f32)], axis=1)
            apart = apart.astype(bf16)
            for k in range(NCLASS):
                wd[k, pl.ds(start, 16), :] = apart[k * 16 : (k + 1) * 16, :]
        return carry

    lax.fori_loop(0, 7, unmix_step, 0)

    cp_idx.wait()
    raw = idx_vmem[...]
    rel = jnp.clip(raw - (box - 1) * (8 * LEAF), 0, LEAF_ROWS - 1)
    row = (rel // LEAF) * LEAF + (rel % 8) * 32 + (rel // 8 % 8) * 4 + rel % LEAF // 64
    idx_vmem[...] = jnp.where(raw < 0, LEAF_ROWS, row)
    cp_smem = local(5, idx_vmem, idx)
    cp_smem.start()

    for cp in coarse_z:
        cp.wait_recv()
    for cp in coarse_x:
        cp.start()
    leaf_first_b[3].start()
    leaf_first_b[4].start()
    leaf_first_b[2].start()
    leaf_first[0].wait_recv()
    leaf_second[0].start()
    leaf_second[1].start()
    leaf_first[1].wait_recv()
    leaf_second[2].start()
    leaf_second[3].start()
    for ((_, dz), (dx, _)), cp in zip(NEAR_SECOND, near_second):
        cp.wait_recv()
        near_core[(-dx, dz)].start()
    for cp in near_core.values():
        cp.wait_recv()
    lax.fori_loop(0, 24, features, 0)
    lax.fori_loop(0, 10, tile_and_steps, 0)
    coarse_c[0].wait_recv()

    for k in range(NCLASS):
        for t in range(4):
            g = coarse_source[k, pair * 4 + t]
            home, member = g >> 5, (g >> 2) & 7
            place = (member & 1) * 256 + home * 16 + (member >> 1) * 4 + (g & 3)
            place = jnp.where(g < 0, COARSE_ROWS, place)
            gat[pl.ds((k * 4 + t) * 4, 4), :] = coarse_tab[place].astype(f32)
    picked = [gat[pl.ds(c, 64, stride=4), :] for c in range(4)]
    picked = jnp.concatenate(picked, axis=1)
    picked = jnp.concatenate([picked, picked], axis=0).astype(bf16)
    picked_ref[...] = picked

    def tile_and_m2l(i, carry):
        start = jnp.minimum(i * 1776, NCLASS * COEF - 1776)
        start = pl.multiple_of(start, 16)
        product(m2l, start, 1776, picked_ref[:, :COEF], NT)
        return tile_and_steps(i + 10, carry)

    lax.fori_loop(0, 4, tile_and_m2l, 0)
    total = None
    for k in range(NCLASS):
        part = tall[pl.ds(k, COEF, stride=NCLASS), :]
        part = jnp.where(lane % 64 // 4 == k, part, 0.0)
        total = part if total is None else total + part
    for shift in (32, 16, 8, 4):
        total = total + pltpu.roll(total, shift, 1)

    cp_l2l.wait()
    right = total.astype(bf16)
    for i, (start, size) in enumerate([(0, 1776), (1776, 8 * COEF - 1776)]):
        product(l2l, start, size, right, NN)
    near_tile(14, 0)
    for i, share in enumerate([(-1, 3), (1, 3), (-1, 1), (1, 1)]):
        leaf_second_b[i].wait_recv()
        leaf_core[share].start()
    total = None
    for o in range(8):
        part = tall[pl.ds(o, COEF, stride=8), :]
        part = jnp.where(lane % 32 // 4 == o, part, 0.0)
        total = part if total is None else total + part
    right = total.astype(bf16)
    for i, (start, size) in enumerate([(0, 1776), (1776, 8 * COEF - 1776)]):
        product(l2l, start, size, right, NN)
    near_tile(15, 0)
    leaf_third[0].wait_recv()
    leaf_third[2].wait_recv()
    leaf_core[(-1, 2)].start()
    leaf_third[1].wait_recv()
    leaf_third[3].wait_recv()
    leaf_core[(1, 2)].start()
    acc[...] = jnp.zeros((448, LEAF), f32)
    for side in range(2):
        total = None
        for o in range(4):
            part = tall[pl.ds(side * 4 + o, COEF, stride=8), :]
            part = jnp.where(lane // 32 == o, part, 0.0)
            total = part if total is None else total + part
        acc[pl.ds(0, COEF), pl.ds(side * TILE, TILE)] = total

    cp_smem.wait()
    for cp in leaf_core.values():
        cp.wait_recv()

    def gather(k, into_ref):
        for start in range(0, LEAF, 16):
            values = []
            for j in range(start, start + 16):
                column = (j % 4) * 64 + (j % 32 // 4) * 8 + j // 32
                values.append(leaf_tab[idx[k, column]].astype(f32))
            for j in range(16):
                into_ref[pl.ds((start + j) * 4, 4), :] = values[j]

    def apply(k, from_ref):
        picked = [from_ref[pl.ds(c, LEAF, stride=4), :].astype(bf16) for c in range(4)]
        picked = jnp.concatenate(picked, axis=1)
        acc[...] += lax.dot_general(wd[k], picked, NT, preferred_element_type=f32)

    gather(0, gat)

    def leaf_class(i, carry):
        gather(2 * i + 1, gat_other)
        apply(2 * i, gat)
        gather(lax.rem(2 * i + 2, NCLASS), gat)
        apply(2 * i + 1, gat_other)
        return carry

    lax.fori_loop(0, NCLASS // 2, leaf_class, 0)

    locals_ = jnp.transpose(acc[...], (1, 0)).astype(bf16)[:, :COEF]
    for q in range(8):
        columns = mult[:, q * 256 : (q + 1) * 256]
        product = lax.dot_general(locals_, columns, NN, preferred_element_type=f32)
        for h in range(2):
            i = q * 2 + h
            hit = row_iota == rowidx[i : i + 1, :]
            far = jnp.where(hit, product[:, h * TILE : (h + 1) * TILE], 0.0)
            far = jnp.sum(far, axis=0, keepdims=True)
            out_ref[i : i + 1, :] = near_acc[i : i + 1, :] + far

    copies = near_first + near_second + list(near_core.values())
    copies += leaf_first + leaf_first_b + leaf_second + leaf_second_b + leaf_third
    copies += list(leaf_core.values())
    copies += coarse_z + coarse_x + coarse_y + coarse_c
    for cp in copies:
        cp.wait_send()


def body(
    multipoles, density, pair_centers, pair_exponent, box_of_pair, near_tiles, near_count,
    m2l_source, coarse_source, m2m_ops, l2l_ops, m2l_ops,
):
    def flat(operators):
        return jnp.transpose(operators, (1, 0, 2)).reshape(-1, COEF)

    grid = (TILES, TILE)
    smem = pl.BlockSpec(memory_space=pltpu.SMEM)
    vmem = pl.BlockSpec(memory_space=pltpu.VMEM)
    anywhere = pl.BlockSpec(memory_space=pl.ANY)
    dma = pltpu.SemaphoreType.DMA
    out = pl.pallas_call(
        kernel,
        out_shape=jax.ShapeDtypeStruct(grid, f32),
        in_specs=[smem, smem, smem, anywhere, vmem, vmem, vmem, vmem]
        + [anywhere, anywhere, anywhere, anywhere],
        out_specs=vmem,
        scratch_shapes=[
            pltpu.VMEM((COEF, 2048), bf16),
            pltpu.VMEM((8 * COEF, COEF), bf16),
            pltpu.VMEM((8 * COEF, COEF), bf16),
            pltpu.VMEM((NCLASS * 448, COEF), bf16),
            pltpu.VMEM((NCLASS, LEAF), jnp.int32),
            pltpu.SMEM((NCLASS, LEAF), jnp.int32),
            pltpu.VMEM((24, 5, TILES, TILE), f32),
            pltpu.VMEM((24 * TILES, 8, TILE), f32),
            pltpu.VMEM((LEAF_ROWS + ZERO_PAD, 4, TILE), bf16),
            pltpu.VMEM((COARSE_ROWS + ZERO_PAD, 4, TILE), bf16),
            pltpu.VMEM((LEAF, 4, TILE), f32),
            pltpu.VMEM((LEAF, 2048), bf16),
            pltpu.VMEM(grid, jnp.int32),
            pltpu.VMEM((2, 8 * COEF, TILE), f32),
            pltpu.VMEM((NCLASS * COEF, TILE), f32),
            pltpu.VMEM((NCLASS, 448, 512), bf16),
            pltpu.VMEM((1024, TILE), f32),
            pltpu.VMEM((1024, TILE), f32),
            pltpu.VMEM((448, LEAF), f32),
            pltpu.VMEM(grid, f32),
            pltpu.VMEM((TILE, 512), bf16),
            dma((6,)),
            dma((23,)), dma((23,)), dma((33,)), dma((33,)), dma((10,)), dma((10,)),
        ],
        compiler_params=pltpu.CompilerParams(
            collective_id=0, has_side_effects=True, vmem_limit_bytes=60 * 1024 * 1024
        ),
    )(
        near_tiles, near_count, jnp.transpose(coarse_source), multipoles,
        density.reshape(grid), pair_centers, pair_exponent.reshape(grid),
        box_of_pair.reshape(grid), jnp.transpose(m2l_source),
        flat(m2m_ops), flat(l2l_ops), flat(m2l_ops),
    )
    return out.reshape(-1)


def solution(mesh):
    return jax.shard_map(
        body,
        mesh=mesh,
        in_specs=(
            P(None, ("box", "pair")),
            P(("box", "pair")),
            P(None, ("box", "pair")),
            P(("box", "pair")),
            P(("box", "pair")),
            P(("box", "pair"), None),
            P(("box", "pair")),
            P("box", None),
            P("box", None),
            P(),
            P(),
            P(),
        ),
        out_specs=P(("box", "pair")),
        check_vma=False,
    )
```

```python
import jax
import jax.numpy as jnp
from jax import lax
from jax.experimental import pallas as pl
from jax.experimental.pallas import tpu as pltpu
from jax.sharding import PartitionSpec as P

MESH = pl.DeviceIdType.MESH
NT = (((1,), (1,)), ((), ()))
NN = (((1,), (0,)), ((), ()))
TILE = 128
TILES = 16
NNEAR = 24
COEF = 441
LEAF = 256
NCLASS = 16
BOXES = 16
LEAF_ROWS = 24 * LEAF
COARSE_ROWS = 512
ZERO_PAD = 16
CHUNK = 1184
f32, bf16 = jnp.float32, jnp.bfloat16

HOPS = [(0, 1), (0, 3), (1, 0), (-1, 0), (0, 2)]
NEAR_SECOND = [((0, dz), (dx, 0)) for dz in (3, 1, 2) for dx in (1, -1)]
OWN = (0, 0)
FIRST = [(OWN, (0, 1), 0), (OWN, (0, 3), 1), (OWN, (1, 0), 0), (OWN, (-1, 0), 0)]
FIRST_B = [(OWN, (0, 1), 1), (OWN, (0, 3), 0), (OWN, (0, 2), None)]
FIRST_B += [(OWN, (1, 0), 1), (OWN, (-1, 0), 1)]
SECOND = [((0, 3), (1, 0), 0), ((0, 3), (-1, 0), 0), ((0, 1), (1, 0), 1), ((0, 1), (-1, 0), 1)]
SECOND_B = [((0, 3), (1, 0), 1), ((0, 3), (-1, 0), 1), ((0, 1), (1, 0), 0), ((0, 1), (-1, 0), 0)]
THIRD = [((-1, 3), (0, 1), 0), ((1, 3), (0, 1), 0), ((-1, 1), (0, 3), 1), ((1, 1), (0, 3), 1)]
ALL_SHARES = [(dx, dz) for dx in (-1, 0, 1) for dz in range(4)]


def split3(values):
    high = values.astype(bf16).astype(f32)
    rest = values - high
    middle = rest.astype(bf16).astype(f32)
    return high, middle, rest - middle


def kernel(
    near_tiles, near_count, coarse_source, mult_hbm, dens_ref, cent_ref, expo_ref, box_ref,
    m2l_source, m2m_hbm, l2l_hbm, m2l_hbm, out_ref,
    mult, m2m, l2l, m2l, idx_vmem, idx, near_tab, feat, leaf_tab, coarse_tab, sc3, onehot, rowidx,
    wide, tall, wd, gat, gat_other, acc, near_acc, picked_ref,
    loc_sem, near_send, near_recv, leaf_send, leaf_recv, coarse_send, coarse_recv,
):
    box = lax.axis_index("box")
    pair = lax.axis_index("pair")
    y, x = box // 4, box % 4
    z, core = pair // 2, pair % 2

    def slot_of(dx, dz, which):
        return (dx + 1) * 8 + ((z + dz) % 4) * 2 + which

    def near_device(ndx, ndz, flip=0):
        other = core if not flip else 1 - core
        return ((box + ndx + BOXES) % BOXES, ((z + ndz) % 4) * 2 + other)

    def plane_device(dy, dx, dz):
        return (((y + dy) % 4) * 4 + (x + dx) % 4, ((z + dz) % 4) * 2 + core)

    def local(i, src, dst):
        return pltpu.make_async_copy(src, dst, loc_sem.at[i])

    own_cols = pl.ds(pl.multiple_of(pair * LEAF, LEAF), LEAF)
    cp_mult = local(0, mult_hbm, mult)
    cp_m2m = local(1, m2m_hbm, m2m)
    cp_m2l = local(2, m2l_hbm, m2l.at[pl.ds(0, NCLASS * COEF)])
    cp_l2l = local(3, l2l_hbm, l2l)
    cp_idx = local(4, m2l_source.at[:, own_cols], idx_vmem)
    cp_mult.start()
    cp_idx.start()
    cp_m2m.start()
    cp_m2l.start()
    cp_l2l.start()

    partners = [near_device(*hop) for hop in HOPS] + [near_device(0, 0, 1)]
    partners += [plane_device(0, d, 0) for d in (1, 2, 3)]
    partners += [plane_device(d, 0, 0) for d in (1, 2, 3)]
    barrier = pltpu.get_barrier_semaphore()
    for device in partners:
        pl.semaphore_signal(barrier, inc=1, device_id=device, device_id_type=MESH)

    own_slot = slot_of(0, 0, core)
    for c in range(3):
        for i in range(TILES):
            row = cent_ref[c : c + 1, i * TILE : (i + 1) * TILE] - 2.0
            near_tab[own_slot, c, i : i + 1, :] = row
    near_tab[own_slot, 3] = 1.0 / expo_ref[...]
    near_tab[own_slot, 4] = dens_ref[...]
    pl.semaphore_wait(barrier, len(partners))

    def near_ref(dx, dz, which):
        return near_tab.at[slot_of(dx, dz, which)]

    def leaf_ref(dx, dz, which, half=None):
        base, size = slot_of(dx, dz, which) * LEAF, LEAF
        if half is not None:
            base, size = base + half * (LEAF // 2), LEAF // 2
        return leaf_tab.at[pl.ds(base, size)]

    def near_copy(i, share, hop, flip=0):
        (dx, dz), (ndx, ndz) = share, hop
        return pltpu.make_async_remote_copy(
            src_ref=near_ref(dx, dz, core),
            dst_ref=near_tab.at[(dx - ndx + 1) * 8 + ((z + dz) % 4) * 2 + core],
            send_sem=near_send.at[i], recv_sem=near_recv.at[i],
            device_id=near_device(ndx, ndz, flip), device_id_type=MESH,
        )

    def leaf_copy(i, share, hop, half=None, flip=0):
        (dx, dz), (ndx, ndz) = share, hop
        return pltpu.make_async_remote_copy(
            src_ref=leaf_ref(dx, dz, core, half), dst_ref=leaf_ref(dx - ndx, dz, core, half),
            send_sem=leaf_send.at[i], recv_sem=leaf_recv.at[i],
            device_id=near_device(ndx, ndz, flip), device_id_type=MESH,
        )

    near_first = [near_copy(i, OWN, hop) for i, hop in enumerate(HOPS)]
    near_second = [near_copy(5 + i, *t) for i, t in enumerate(NEAR_SECOND)]
    near_core = {s: near_copy(11 + i, s, OWN, 1) for i, s in enumerate(ALL_SHARES)}
    leaf_first = [leaf_copy(i, *t) for i, t in enumerate(FIRST)]
    leaf_first_b = [leaf_copy(4 + i, *t) for i, t in enumerate(FIRST_B)]
    leaf_second = [leaf_copy(9 + i, *t) for i, t in enumerate(SECOND)]
    leaf_second_b = [leaf_copy(13 + i, *t) for i, t in enumerate(SECOND_B)]
    leaf_third = [leaf_copy(17 + i, *t) for i, t in enumerate(THIRD)]
    leaf_core = {s: leaf_copy(21 + i, s, OWN, None, 1) for i, s in enumerate(ALL_SHARES)}

    for cp in near_first:
        cp.start()
    near_core[(0, 0)].start()

    local_box = box_ref[...] - (box * (8 * LEAF) + pair * LEAF)
    rowidx[...] = (local_box % 8) * 32 + (local_box // 8 % 8) * 4 + local_box // 64
    row_iota = lax.broadcasted_iota(jnp.int32, (LEAF, TILE), 0)
    for i in range(TILES):
        weight = dens_ref[i : i + 1, :].astype(bf16).astype(f32)
        hit = row_iota == rowidx[i : i + 1, :]
        onehot[:, i * TILE : (i + 1) * TILE] = jnp.where(hit, weight, 0.0).astype(bf16)
    leaf_tab[pl.ds(LEAF_ROWS, ZERO_PAD)] = jnp.zeros((ZERO_PAD, 4, TILE), bf16)
    coarse_tab[pl.ds(COARSE_ROWS, ZERO_PAD)] = jnp.zeros((ZERO_PAD, 4, TILE), bf16)
    cp_mult.wait()
    leaf = lax.dot_general(onehot[...], mult[...], NT, preferred_element_type=f32)
    leaf = jnp.concatenate([leaf, jnp.zeros((LEAF, 512 - COEF), f32)], axis=1)
    for c in range(4):
        sc3[:, c, :] = leaf[:, c * TILE : (c + 1) * TILE]
    leaf_tab[pl.ds(own_slot * LEAF, LEAF)] = sc3[...].astype(bf16)

    def product(operators, start, size, right, dims):
        rows = operators[pl.ds(start, size), :]
        result = lax.dot_general(rows, right, dims, preferred_element_type=f32)
        if result.shape[1] == 256:
            wide[0, pl.ds(start, size), :] = result[:, :TILE]
            wide[1, pl.ds(start, size), :] = result[:, TILE:]
        else:
            tall[pl.ds(start, size), :] = result

    def stream(operators, total, right, dims):
        def step(i, carry):
            product(operators, pl.multiple_of(i * CHUNK, CHUNK), CHUNK, right, dims)
            return carry

        whole = total // CHUNK
        lax.fori_loop(0, whole, step, 0)
        if total % CHUNK:
            product(operators, whole * CHUNK, total % CHUNK, right, dims)

    lane = lax.broadcasted_iota(jnp.int32, (COEF, TILE), 1)

    leaf_first[0].start()
    leaf_first[1].start()
    leaf_core[(0, 0)].start()

    cp_m2m.wait()
    stream(m2m, 8 * COEF, leaf[:, :COEF].astype(bf16), NT)
    total = None
    for o in range(8):
        part = wide[o // 4, pl.ds(o, COEF, stride=8), :]
        part = jnp.where(lane // 32 == o % 4, part, 0.0)
        total = part if total is None else total + part
    total = total + pltpu.roll(total, 64, 1)
    total = total + pltpu.roll(total, 32, 1)
    for j, dz in enumerate((3, 1, 2)):
        near_first[(0, 1, 4)[j]].wait_recv()
        near_second[2 * j].start()
        near_second[2 * j + 1].start()
        near_core[(0, dz)].start()
    leaf_first[2].start()
    leaf_first[3].start()
    stream(m2m, 8 * COEF, total.astype(bf16), NN)
    total = None
    for o in range(8):
        part = tall[pl.ds(o, COEF, stride=8), :]
        part = jnp.where(lane % 32 // 4 == o, part, 0.0)
        total = part if total is None else total + part
    for shift in (16, 8, 4):
        total = total + pltpu.roll(total, shift, 1)
    coarse = jnp.concatenate([total, jnp.zeros((512 - COEF, TILE), f32)], axis=0)
    coarse = jnp.transpose(coarse, (1, 0))
    for c in range(4):
        sc3[0:4, c, :] = coarse[0:4, c * TILE : (c + 1) * TILE]
    core_base, y_base, x_base = core * 256, y * 64, x * 16
    coarse_tab[pl.ds(core_base + y_base + x_base + z * 4, 4)] = sc3[0:4].astype(bf16)

    def coarse_copy(i, base, size, device):
        return pltpu.make_async_remote_copy(
            src_ref=coarse_tab.at[pl.ds(base, size)], dst_ref=coarse_tab.at[pl.ds(base, size)],
            send_sem=coarse_send.at[i], recv_sem=coarse_recv.at[i],
            device_id=device, device_id_type=MESH,
        )

    coarse_z = [
        coarse_copy(i, core_base + y_base + x_base + z * 4, 4, plane_device(0, 0, i + 1))
        for i in range(3)
    ]
    coarse_x = [
        coarse_copy(3 + i, core_base + y_base + x_base, 16, plane_device(0, i + 1, 0))
        for i in range(3)
    ]
    coarse_y = [
        coarse_copy(6 + i, core_base + y_base, 64, plane_device(i + 1, 0, 0)) for i in range(3)
    ]
    coarse_c = [coarse_copy(9, core_base, 256, near_device(0, 0, 1))]
    for cp in coarse_z:
        cp.start()
    leaf_first_b[0].start()
    leaf_first_b[1].start()
    near_first[2].wait_recv()
    near_core[(-1, 0)].start()
    near_first[3].wait_recv()
    near_core[(1, 0)].start()

    def features(s, carry):
        px, py, pz = near_tab[s, 0], near_tab[s, 1], near_tab[s, 2]
        rows = [px, py, pz, px * px + py * py + pz * pz, jnp.ones_like(px)]
        rows += [near_tab[s, 3], near_tab[s, 4], jnp.zeros_like(px)]
        for r, value in enumerate(rows):
            feat[pl.ds(s * TILES, TILES), r, :] = value
        return carry


    def near_tile(u, carry):
        own = feat[own_slot * TILES + u]
        row = lax.broadcasted_iota(jnp.int32, (8, TILE), 0)
        left = jnp.where(row < 3, -2.0 * own, 0.0)
        left = jnp.where(row == 3, 1.0, left)
        left = jnp.where(row == 4, own[3:4, :], left)
        high, middle, low = split3(left)
        left = jnp.concatenate([high, middle, low, high, middle, high], axis=0)
        left = jnp.transpose(left, (1, 0)).astype(bf16)
        inverse = jnp.transpose(jnp.broadcast_to(own[5:6, :], (TILE, TILE)), (1, 0))
        count = near_count[u]

        def one(k):
            tile = near_tiles[u, k] - (box - 1) * (TILES * 8)
            tile = jnp.where(k < count, tile, 0)
            source = feat[tile]
            high, middle, low = split3(source)
            right = jnp.concatenate([high, high, high, middle, middle, low], axis=0).astype(bf16)
            square = lax.dot_general(left, right, NN, preferred_element_type=f32)
            square = jnp.maximum(square, 1e-9)
            weight = jnp.where(k < count, source[6:7, :], 0.0)
            scale = lax.rsqrt(inverse + source[5:6, :])
            reciprocal = lax.rsqrt(square)
            return lax.erf(square * reciprocal * scale) * (reciprocal * weight)

        total = jnp.zeros((TILE, TILE), f32)
        for k in range(NNEAR):
            total = total + one(k)
        near_acc[pl.ds(u, 1), :] = jnp.transpose(jnp.sum(total, axis=1, keepdims=True), (1, 0))
        return carry


    def steps_between(u):
        @pl.when(u == 3)
        def _():
            leaf_first_b[0].wait_recv()
            leaf_second_b[0].start()
            leaf_second_b[1].start()
            leaf_core[(0, 3)].start()
            leaf_first_b[1].wait_recv()
            leaf_second_b[2].start()
            leaf_second_b[3].start()
            leaf_core[(0, 1)].start()

        @pl.when(u == 4)
        def _():
            for cp in coarse_x:
                cp.wait_recv()
            for cp in coarse_y:
                cp.start()

        @pl.when(u == 7)
        def _():
            for cp in coarse_y:
                cp.wait_recv()
            coarse_c[0].start()

        @pl.when(u == 11)
        def _():
            for i, dx in enumerate((-1, 1)):
                leaf_first[2 + i].wait_recv()
                leaf_first_b[3 + i].wait_recv()
                leaf_core[(dx, 0)].start()
            for i in range(4):
                leaf_second[i].wait_recv()
                leaf_third[i].start()
            leaf_first_b[2].wait_recv()
            leaf_core[(0, 2)].start()

    def tile_and_steps(u, carry):
        near_tile(u, carry)
        steps_between(u)
        return carry

    cp_m2l.wait()
    m2l[pl.ds(NCLASS * COEF, NCLASS * 7), :] = jnp.zeros((NCLASS * 7, COEF), bf16)
    into = lax.broadcasted_iota(jnp.int32, (256, 256), 0)
    outof = lax.broadcasted_iota(jnp.int32, (256, 256), 1)
    permute = (outof == into % 16 * NCLASS + into // 16).astype(f32).astype(bf16)

    def unmix_step(i, carry):
        for j in range(4):
            start = pl.multiple_of((i * 4 + j) * 16, 16)
            rows = m2l[pl.ds(pl.multiple_of(start * NCLASS, 256), 256), :]
            apart = lax.dot_general(permute, rows, NN, preferred_element_type=f32)
            apart = jnp.concatenate([apart, jnp.zeros((256, 512 - COEF), f32)], axis=1)
            apart = apart.astype(bf16)
            for k in range(NCLASS):
                wd[k, pl.ds(start, 16), :] = apart[k * 16 : (k + 1) * 16, :]
        return carry

    lax.fori_loop(0, 7, unmix_step, 0)

    cp_idx.wait()
    raw = idx_vmem[...]
    rel = jnp.clip(raw - (box - 1) * (8 * LEAF), 0, LEAF_ROWS - 1)
    row = (rel // LEAF) * LEAF + (rel % 8) * 32 + (rel // 8 % 8) * 4 + rel % LEAF // 64
    idx_vmem[...] = jnp.where(raw < 0, LEAF_ROWS, row)
    cp_smem = local(5, idx_vmem, idx)
    cp_smem.start()

    for cp in coarse_z:
        cp.wait_recv()
    for cp in coarse_x:
        cp.start()
    leaf_first_b[3].start()
    leaf_first_b[4].start()
    leaf_first_b[2].start()
    leaf_first[0].wait_recv()
    leaf_second[0].start()
    leaf_second[1].start()
    leaf_first[1].wait_recv()
    leaf_second[2].start()
    leaf_second[3].start()
    for ((_, dz), (dx, _)), cp in zip(NEAR_SECOND, near_second):
        cp.wait_recv()
        near_core[(-dx, dz)].start()
    for cp in near_core.values():
        cp.wait_recv()
    lax.fori_loop(0, 24, features, 0)
    lax.fori_loop(0, 12, tile_and_steps, 0)
    coarse_c[0].wait_recv()

    for k in range(NCLASS):
        for t in range(4):
            g = coarse_source[k, pair * 4 + t]
            home, member = g >> 5, (g >> 2) & 7
            place = (member & 1) * 256 + home * 16 + (member >> 1) * 4 + (g & 3)
            place = jnp.where(g < 0, COARSE_ROWS, place)
            gat[pl.ds((k * 4 + t) * 4, 4), :] = coarse_tab[place].astype(f32)
    picked = [gat[pl.ds(c, 64, stride=4), :] for c in range(4)]
    picked = jnp.concatenate(picked, axis=1)
    picked = jnp.concatenate([picked, picked], axis=0).astype(bf16)
    picked_ref[...] = picked

    def tile_and_m2l(i, carry):
        start = jnp.minimum(i * 1776, NCLASS * COEF - 1776)
        start = pl.multiple_of(start, 16)
        product(m2l, start, 1776, picked_ref[:, :COEF], NT)
        return tile_and_steps(i + 12, carry)

    lax.fori_loop(0, 4, tile_and_m2l, 0)
    total = None
    for k in range(NCLASS):
        part = tall[pl.ds(k, COEF, stride=NCLASS), :]
        part = jnp.where(lane % 64 // 4 == k, part, 0.0)
        total = part if total is None else total + part
    for shift in (32, 16, 8, 4):
        total = total + pltpu.roll(total, shift, 1)

    cp_l2l.wait()
    right = total.astype(bf16)
    for i, (start, size) in enumerate([(0, 1776), (1776, 8 * COEF - 1776)]):
        product(l2l, start, size, right, NN)
    for i, share in enumerate([(-1, 3), (1, 3), (-1, 1), (1, 1)]):
        leaf_second_b[i].wait_recv()
        leaf_core[share].start()
    total = None
    for o in range(8):
        part = tall[pl.ds(o, COEF, stride=8), :]
        part = jnp.where(lane % 32 // 4 == o, part, 0.0)
        total = part if total is None else total + part
    right = total.astype(bf16)
    for i, (start, size) in enumerate([(0, 1776), (1776, 8 * COEF - 1776)]):
        product(l2l, start, size, right, NN)
    leaf_third[0].wait_recv()
    leaf_third[2].wait_recv()
    leaf_core[(-1, 2)].start()
    leaf_third[1].wait_recv()
    leaf_third[3].wait_recv()
    leaf_core[(1, 2)].start()
    acc[...] = jnp.zeros((448, LEAF), f32)
    for side in range(2):
        total = None
        for o in range(4):
            part = tall[pl.ds(side * 4 + o, COEF, stride=8), :]
            part = jnp.where(lane // 32 == o, part, 0.0)
            total = part if total is None else total + part
        acc[pl.ds(0, COEF), pl.ds(side * TILE, TILE)] = total

    cp_smem.wait()
    for cp in leaf_core.values():
        cp.wait_recv()

    def gather(k, into_ref):
        for start in range(0, LEAF, 16):
            values = []
            for j in range(start, start + 16):
                column = (j % 4) * 64 + (j % 32 // 4) * 8 + j // 32
                values.append(leaf_tab[idx[k, column]].astype(f32))
            for j in range(16):
                into_ref[pl.ds((start + j) * 4, 4), :] = values[j]

    def apply(k, from_ref):
        picked = [from_ref[pl.ds(c, LEAF, stride=4), :].astype(bf16) for c in range(4)]
        picked = jnp.concatenate(picked, axis=1)
        acc[...] += lax.dot_general(wd[k], picked, NT, preferred_element_type=f32)

    gather(0, gat)

    def leaf_class(i, carry):
        gather(2 * i + 1, gat_other)
        apply(2 * i, gat)
        gather(lax.rem(2 * i + 2, NCLASS), gat)
        apply(2 * i + 1, gat_other)
        return carry

    lax.fori_loop(0, NCLASS // 2, leaf_class, 0)

    locals_ = jnp.transpose(acc[...], (1, 0)).astype(bf16)[:, :COEF]
    for q in range(8):
        columns = mult[:, q * 256 : (q + 1) * 256]
        product = lax.dot_general(locals_, columns, NN, preferred_element_type=f32)
        for h in range(2):
            i = q * 2 + h
            hit = row_iota == rowidx[i : i + 1, :]
            far = jnp.where(hit, product[:, h * TILE : (h + 1) * TILE], 0.0)
            far = jnp.sum(far, axis=0, keepdims=True)
            out_ref[i : i + 1, :] = near_acc[i : i + 1, :] + far

    copies = near_first + near_second + list(near_core.values())
    copies += leaf_first + leaf_first_b + leaf_second + leaf_second_b + leaf_third
    copies += list(leaf_core.values())
    copies += coarse_z + coarse_x + coarse_y + coarse_c
    for cp in copies:
        cp.wait_send()


def body(
    multipoles, density, pair_centers, pair_exponent, box_of_pair, near_tiles, near_count,
    m2l_source, coarse_source, m2m_ops, l2l_ops, m2l_ops,
):
    def flat(operators):
        return jnp.transpose(operators, (1, 0, 2)).reshape(-1, COEF)

    grid = (TILES, TILE)
    smem = pl.BlockSpec(memory_space=pltpu.SMEM)
    vmem = pl.BlockSpec(memory_space=pltpu.VMEM)
    anywhere = pl.BlockSpec(memory_space=pl.ANY)
    dma = pltpu.SemaphoreType.DMA
    out = pl.pallas_call(
        kernel,
        out_shape=jax.ShapeDtypeStruct(grid, f32),
        in_specs=[smem, smem, smem, anywhere, vmem, vmem, vmem, vmem]
        + [anywhere, anywhere, anywhere, anywhere],
        out_specs=vmem,
        scratch_shapes=[
            pltpu.VMEM((COEF, 2048), bf16),
            pltpu.VMEM((8 * COEF, COEF), bf16),
            pltpu.VMEM((8 * COEF, COEF), bf16),
            pltpu.VMEM((NCLASS * 448, COEF), bf16),
            pltpu.VMEM((NCLASS, LEAF), jnp.int32),
            pltpu.SMEM((NCLASS, LEAF), jnp.int32),
            pltpu.VMEM((24, 5, TILES, TILE), f32),
            pltpu.VMEM((24 * TILES, 8, TILE), f32),
            pltpu.VMEM((LEAF_ROWS + ZERO_PAD, 4, TILE), bf16),
            pltpu.VMEM((COARSE_ROWS + ZERO_PAD, 4, TILE), bf16),
            pltpu.VMEM((LEAF, 4, TILE), f32),
            pltpu.VMEM((LEAF, 2048), bf16),
            pltpu.VMEM(grid, jnp.int32),
            pltpu.VMEM((2, 8 * COEF, TILE), f32),
            pltpu.VMEM((NCLASS * COEF, TILE), f32),
            pltpu.VMEM((NCLASS, 448, 512), bf16),
            pltpu.VMEM((1024, TILE), f32),
            pltpu.VMEM((1024, TILE), f32),
            pltpu.VMEM((448, LEAF), f32),
            pltpu.VMEM(grid, f32),
            pltpu.VMEM((TILE, 512), bf16),
            dma((6,)),
            dma((23,)), dma((23,)), dma((33,)), dma((33,)), dma((10,)), dma((10,)),
        ],
        compiler_params=pltpu.CompilerParams(
            collective_id=0, has_side_effects=True, vmem_limit_bytes=60 * 1024 * 1024
        ),
    )(
        near_tiles, near_count, jnp.transpose(coarse_source), multipoles,
        density.reshape(grid), pair_centers, pair_exponent.reshape(grid),
        box_of_pair.reshape(grid), jnp.transpose(m2l_source),
        flat(m2m_ops), flat(l2l_ops), flat(m2l_ops),
    )
    return out.reshape(-1)


def solution(mesh):
    return jax.shard_map(
        body,
        mesh=mesh,
        in_specs=(
            P(None, ("box", "pair")),
            P(("box", "pair")),
            P(None, ("box", "pair")),
            P(("box", "pair")),
            P(("box", "pair")),
            P(("box", "pair"), None),
            P(("box", "pair")),
            P("box", None),
            P("box", None),
            P(),
            P(),
            P(),
        ),
        out_specs=P(("box", "pair")),
        check_vma=False,
    )
```
